512 devices in a mesh: dp: 64 (over z, y), tensor: 8 (over x, core).
Axes of the slice: x: 4, y: 8, z: 8, core: 2. Of those that a mesh axis runs over, the one named last changes fastest.
Arguments:
- cache_keys: bfloat16 [3072, 128, 1024], P('dp', None, 'tensor'), may hold values from -5 to 5
- cache_values: bfloat16 [3072, 128, 1024], P('dp', None, 'tensor'), may hold values from -24 to 24
- lengths: int32 [3072], P('dp'), may hold values from 2 to 128, as said below
- queries: bfloat16 [4, 3072, 8192], P(None, 'dp', 'tensor'), may hold values from -125 to 125
- new_keys: bfloat16 [4, 3072, 1024], P(None, 'dp', 'tensor'), may hold values from -9 to 9
- new_values: bfloat16 [4, 3072, 1024], P(None, 'dp', 'tensor'), may hold values from -72 to 72
- reward_weight: bfloat16 [8192], P('tensor'), may hold values from -0.119628906 to 0.119628906
- kept_candidates: int32 [64, 32], P('dp'), may hold values from 0 to 47, as said below
- arrival_cohort: int32 [64, 32], P('dp'), may hold values from 0 to 63, as said below
- arrival_place: int32 [64, 32], P('dp'), may hold values from 0 to 31, as said below
Outputs:
- early_out: bfloat16 [2, 3072, 8192], P(None, 'dp', 'tensor')
- reward: float32 [3072], P('dp')
- late_out: bfloat16 [2, 2048, 8192], P(None, 'dp', 'tensor')
The draws below stay inside these ranges and needn't reach their ends.
Inputs may be any that keep to these rules, and one draw needn't show every extreme that they name: `kept_candidates`: each row names 32 different candidates of its prompt, in ascending order. `arrival_cohort`: every pair of group and slot receives exactly one survivor. One prompt sends at most 1 survivors to one group, and exactly 1 to some group. `arrival_place`: see arrival_cohort. `lengths`: some candidate holds the full 128 tokens.
All inputs are finite; a program needn't handle non-finite values.
Results may differ from the reference program's by a relative error of at most 0.009.
Values may be sent and summed in bfloat16 or wider, within the bound.
A program may use at most 64 MiB of HBM per device.

```python
import math
import jax
import jax.numpy as jnp
from jax import lax

QH = 64
KVH = 8
HD = 128
WINNER_PLACES = 32
CACHE = 128
STEPS = 2
OPTION_TOTAL = 48
QUERY_AMOUNT = 64
CAND = 3072
SURV = 2048


def anchor_rows(key):
    return jnp.clip(jax.random.normal(key, (CAND, KVH * HD), jnp.float32), -5.0, 5.0)


def routing_tables(key):
    primary_order_key, second_key, tertiary_sort_value = jax.random.split(key, 3)
    relabel_elements = jax.random.permutation(primary_order_key, QUERY_AMOUNT).astype(jnp.int32)
    backward_arrangement = jnp.argsort(relabel_elements).astype(jnp.int32)
    opening_gaps_list = jax.random.permutation(second_key, QUERY_AMOUNT).astype(jnp.int32)
    champion_spot_number_here = jnp.arange(WINNER_PLACES, dtype=jnp.int32)
    goal_batch_part = relabel_elements[(backward_arrangement[:, None] + opening_gaps_list[champion_spot_number_here % QUERY_AMOUNT][None, :]) % QUERY_AMOUNT]
    circular_rotation = jax.random.randint(tertiary_sort_value, (QUERY_AMOUNT,), 0, WINNER_PLACES).astype(jnp.int32)
    target_place = (champion_spot_number_here[None, :] + circular_rotation[goal_batch_part]) % WINNER_PLACES
    return (goal_batch_part.astype(jnp.int32), target_place.astype(jnp.int32))


def draw_cache_keys(key, part):
    anchors = anchor_rows(key)
    key = jax.random.fold_in(key, 7)
    filled = jnp.clip(jax.random.normal(key, (CAND, CACHE, KVH * HD), jnp.float32), -5.0, 5.0)
    filled = filled.at[:, 0].set(anchors)
    return filled.astype(jnp.bfloat16)


def draw_queries(key, part):
    key = jax.random.fold_in(key, 9)
    filled = jnp.clip(jax.random.normal(key, (2 * STEPS, CAND, QH * HD), jnp.float32), -5.0, 5.0)
    return filled.astype(jnp.bfloat16)


def draw_lengths(key, part):
    key = jax.random.fold_in(key, 5)
    primary_order_key, second_key = jax.random.split(key)
    drawn = jax.random.randint(primary_order_key, (QUERY_AMOUNT, OPTION_TOTAL), 2, CACHE + 1).astype(jnp.int32)
    fullest = jax.random.randint(second_key, (QUERY_AMOUNT,), 0, OPTION_TOTAL).astype(jnp.int32)
    column_ids = jnp.arange(OPTION_TOTAL, dtype=jnp.int32)[None, :]
    drawn = jnp.where(column_ids == fullest[:, None], CACHE, drawn)
    return drawn.reshape(CAND).astype(jnp.int32)


def draw_kept_candidates(key, part):
    key = jax.random.fold_in(key, 4)
    row_keys = jax.random.split(key, QUERY_AMOUNT)

    def one_prompt(entry_sort_value):
        return jnp.sort(jax.random.permutation(entry_sort_value, OPTION_TOTAL)[:WINNER_PLACES])
    return jax.vmap(one_prompt)(row_keys).astype(jnp.int32)


def draw_arrival_cohort(key, part):
    goal_batch_part, target_place = routing_tables(key)
    return goal_batch_part


def draw_arrival_place(key, part):
    goal_batch_part, target_place = routing_tables(key)
    return target_place


def block_levels(own_key, extent, cuts, low, high):
    gain, own = 1.0, jax.random.fold_in(own_key, 6)
    for axis_at, blocks in cuts:
        heights = jnp.exp(jax.random.uniform(jax.random.fold_in(own, axis_at), (blocks,), jnp.float32, low / len(cuts), high / len(cuts)))
        gain = gain * jnp.repeat(heights, extent[axis_at] // blocks).reshape([-1 if axis == axis_at else 1 for axis in range(len(extent))])
    return gain


def gaussian(own_key, extent, spread, bound, pieces=(), kind=jnp.bfloat16):
    entries = spread * jax.random.normal(own_key, extent, jnp.float32)
    if pieces:
        entries = entries * block_levels(own_key, extent, pieces, -0.22, 0.18)
    return jnp.clip(entries, -bound, bound).astype(kind)


def setup_inputs(seed: int = 0) -> dict:
    splits = jax.random.split(jax.random.key(seed), 11)
    cache_keys = draw_cache_keys(jax.random.fold_in(splits[10], 71), 0)
    cache_values = gaussian(splits[1], (CAND, CACHE, KVH * HD), 4.0, 24.0, ((0, 64), (2, 8)))
    lengths = draw_lengths(jax.random.fold_in(splits[10], 71), 0)
    queries = draw_queries(jax.random.fold_in(splits[10], 71), 0)
    new_keys = gaussian(splits[4], (2 * STEPS, CAND, KVH * HD), 1.5, 9.0, ((1, 64), (2, 8)))
    new_values = gaussian(splits[5], (2 * STEPS, CAND, KVH * HD), 12.0, 72.0, ((1, 64), (2, 8)))
    reward_weight = gaussian(splits[6], (QH * HD,), 0.02, 0.119628906, ((0, 8),))
    kept_candidates = draw_kept_candidates(jax.random.fold_in(splits[10], 71), 0)
    arrival_cohort = draw_arrival_cohort(jax.random.fold_in(splits[10], 71), 0)
    arrival_place = draw_arrival_place(jax.random.fold_in(splits[10], 71), 0)
    return dict(cache_keys=cache_keys, cache_values=cache_values, lengths=lengths, queries=queries, new_keys=new_keys, new_values=new_values, reward_weight=reward_weight, kept_candidates=kept_candidates, arrival_cohort=arrival_cohort, arrival_place=arrival_place)


def attend(queries_now, key_rows, value_rows, live_length, fresh_k, fresh_v):
    rows_count = queries_now.shape[0]
    seen_steps = fresh_k.shape[1]
    group_size = QH // KVH
    query_f = queries_now.astype(jnp.float32).reshape(rows_count, KVH, group_size, HD)
    key_f = key_rows.astype(jnp.float32).reshape(rows_count, CACHE, KVH, HD)
    value_f = value_rows.astype(jnp.float32).reshape(rows_count, CACHE, KVH, HD)
    fresh_kf = fresh_k.astype(jnp.float32).reshape(rows_count, seen_steps, KVH, HD)
    fresh_vf = fresh_v.astype(jnp.float32).reshape(rows_count, seen_steps, KVH, HD)
    score_scale = 1.0 / math.sqrt(HD)
    high = lax.Precision.HIGHEST
    cache_scores = jnp.einsum('bgqd,bpgd->bgqp', query_f, key_f, precision=high) * score_scale
    fresh_scores = jnp.einsum('bgqd,bngd->bgqn', query_f, fresh_kf, precision=high) * score_scale
    live_rows = jnp.arange(CACHE, dtype=jnp.int32)[None, :] < live_length[:, None]
    cache_scores = jnp.where(live_rows[:, None, None, :], cache_scores, -jnp.inf)
    row_top = jnp.maximum(lax.optimization_barrier(jnp.max(cache_scores, axis=-1)), lax.optimization_barrier(jnp.max(fresh_scores, axis=-1)))
    cache_exp = jnp.exp(cache_scores - row_top[..., None])
    fresh_exp = jnp.exp(fresh_scores - row_top[..., None])
    row_total = lax.optimization_barrier(jnp.sum(cache_exp, axis=-1)) + lax.optimization_barrier(jnp.sum(fresh_exp, axis=-1))
    cache_weights = lax.optimization_barrier((cache_exp / row_total[..., None]).astype(jnp.bfloat16)).astype(jnp.float32)
    fresh_weights = lax.optimization_barrier((fresh_exp / row_total[..., None]).astype(jnp.bfloat16)).astype(jnp.float32)
    result = jnp.einsum('bgqp,bpgd->bgqd', cache_weights, value_f, precision=high)
    result = result + jnp.einsum('bgqn,bngd->bgqd', fresh_weights, fresh_vf, precision=high)
    return result.reshape(rows_count, QH * HD).astype(jnp.bfloat16)

def reference(cache_keys, cache_values, lengths, queries, new_keys, new_values, reward_weight, kept_candidates, arrival_cohort, arrival_place):

    def early_block(segment_number):
        offset_rows = segment_number * OPTION_TOTAL
        key_rows = lax.dynamic_slice_in_dim(cache_keys, offset_rows, OPTION_TOTAL, 0)
        value_rows = lax.dynamic_slice_in_dim(cache_values, offset_rows, OPTION_TOTAL, 0)
        live_length = lax.dynamic_slice_in_dim(lengths, offset_rows, OPTION_TOTAL, 0)
        query_rows = lax.dynamic_slice_in_dim(queries, offset_rows, OPTION_TOTAL, 1)
        fresh_k = jnp.moveaxis(lax.dynamic_slice_in_dim(new_keys, offset_rows, OPTION_TOTAL, 1), 0, 1)
        fresh_v = jnp.moveaxis(lax.dynamic_slice_in_dim(new_values, offset_rows, OPTION_TOTAL, 1), 0, 1)
        results = [attend(query_rows[step_index], key_rows, value_rows, live_length, fresh_k[:, :step_index + 1], fresh_v[:, :step_index + 1]) for step_index in range(STEPS)]
        return jnp.stack(results)
    early_blocks = lax.map(early_block, jnp.arange(QUERY_AMOUNT, dtype=jnp.int32))
    early_out = jnp.moveaxis(early_blocks, 1, 0).reshape(STEPS, CAND, QH * HD)
    reward = lax.optimization_barrier(jnp.sum(early_out[STEPS - 1].astype(jnp.float32) * reward_weight.astype(jnp.float32), axis=-1))
    root = jnp.arange(QUERY_AMOUNT, dtype=jnp.int32)[:, None] * OPTION_TOTAL + kept_candidates
    receiver_index = arrival_cohort * WINNER_PLACES + arrival_place
    sender_index = jnp.zeros((SURV,), jnp.int32).at[receiver_index.reshape(-1)].set(root.reshape(-1))

    def late_block(segment_number):
        selected_entries = lax.dynamic_slice_in_dim(sender_index, segment_number * WINNER_PLACES, WINNER_PLACES, 0)
        key_rows = jnp.take(cache_keys, selected_entries, axis=0)
        value_rows = jnp.take(cache_values, selected_entries, axis=0)
        live_length = jnp.take(lengths, selected_entries, axis=0)
        query_rows = jnp.take(queries, selected_entries, axis=1)
        fresh_k = jnp.moveaxis(jnp.take(new_keys, selected_entries, axis=1), 0, 1)
        fresh_v = jnp.moveaxis(jnp.take(new_values, selected_entries, axis=1), 0, 1)
        results = [attend(query_rows[step_index], key_rows, value_rows, live_length, fresh_k[:, :step_index + 1], fresh_v[:, :step_index + 1]) for step_index in range(STEPS, 2 * STEPS)]
        return jnp.stack(results)
    late_blocks = lax.map(late_block, jnp.arange(QUERY_AMOUNT, dtype=jnp.int32))
    late_out = jnp.moveaxis(late_blocks, 1, 0).reshape(STEPS, SURV, QH * HD)
    return (early_out, reward, late_out)
```

```python
import functools
import math

import jax
import jax.numpy as jnp
from jax import lax
from jax.experimental import pallas as pl
from jax.experimental.pallas import tpu as pltpu
from jax.sharding import PartitionSpec as P

MESH = pl.DeviceIdType.MESH
HD = 128
PAD = 16
BLOCK = 8
RING = 8
NEG = -1e30
NT = (((1,), (1,)), ((), ()))


def all_of(ref, count, sem):
    part = ref.at[pl.ds(0, count)]
    return pltpu.make_async_copy(part, part, sem)


def kernel(
    dims,
    kept_s, lengths_s, cohort_v, place_v, weight_v,
    keys_h, values_h, queries_h, fresh_k_h, fresh_v_h,
    early_h, reward_o, late_h,
    kx, vx, qb, nkb, nvb, qf, nf, of, late_buf, send, recv, stage, late_stage,
    row_v, idx_s, meta_mine, meta_y, meta_all, rw,
    in_sem, row_sem, out_sem, send_sem, recv_sem, my_send, my_recv, mz_send, mz_recv,
    rw_send, rw_recv,
):
    zn, yn, tn, cand, kept_n, heads = dims
    groups = zn * yn
    cache = kx.shape[1] - PAD
    g_me = lax.axis_index("dp")
    t_me = lax.axis_index("tensor")
    z_me, y_me = g_me // yn, g_me % yn

    ins = [
        pltpu.make_async_copy(queries_h, qb, in_sem.at[0]),
        pltpu.make_async_copy(fresh_k_h, nkb, in_sem.at[1]),
        pltpu.make_async_copy(fresh_v_h, nvb, in_sem.at[2]),
        pltpu.make_async_copy(keys_h, kx.at[:, pl.ds(0, cache), :], in_sem.at[3]),
        pltpu.make_async_copy(values_h, vx.at[:, pl.ds(0, cache), :], in_sem.at[4]),
    ]
    for copy in ins:
        copy.start()

    barrier = pltpu.get_barrier_semaphore()

    def greet(d, _):
        pl.semaphore_signal(
            barrier, inc=1, device_id=(lax.rem(g_me + d, groups), t_me), device_id_type=MESH
        )
        return 0

    lax.fori_loop(1, groups, greet, 0)

    def greet_t(d, _):
        pl.semaphore_signal(
            barrier, inc=1, device_id=(g_me, lax.rem(t_me + d, tn)), device_id_type=MESH
        )
        return 0

    lax.fori_loop(1, tn, greet_t, 0)

    eye = lax.broadcasted_iota(jnp.int32, (kept_n, kept_n), 0) == lax.broadcasted_iota(
        jnp.int32, (kept_n, kept_n), 1
    )

    def column(row):
        return jnp.sum(jnp.where(eye, row, 0), axis=1, keepdims=True)

    lane_g = lax.broadcasted_iota(jnp.int32, (kept_n, 128), 1)
    sub_k = lax.broadcasted_iota(jnp.int32, (kept_n, 128), 0)
    hit = column(cohort_v[...]) == lane_g
    chosen = jnp.min(jnp.where(hit, sub_k, kept_n), axis=0, keepdims=True)
    slot_row = jnp.max(jnp.where(hit, column(place_v[...]) + 1, 0), axis=0, keepdims=True)
    row_v[0] = chosen
    to_smem = pltpu.make_async_copy(row_v.at[0], idx_s.at[0], row_sem.at[0])
    to_smem.start()
    meta_mine[...] = jnp.where(
        lax.broadcasted_iota(jnp.int32, (RING, 128), 0) == y_me, slot_row, 0
    )

    pl.semaphore_wait(barrier, groups - 1 + tn - 1)

    def y_copy(d):
        return pltpu.make_async_remote_copy(
            src_ref=meta_mine,
            dst_ref=meta_y.at[y_me],
            send_sem=my_send,
            recv_sem=my_recv,
            device_id=(z_me * yn + lax.rem(y_me + d, yn), t_me),
            device_id_type=MESH,
        )

    lax.fori_loop(1, yn, lambda d, _: (y_copy(d).start(), 0)[1], 0)
    meta_y[y_me] = meta_mine[...]

    for copy in ins[:3]:
        copy.wait()
    steps = qb.shape[0]
    for t in range(steps):
        for h in range(heads):
            qf[pl.ds((t * heads + h) * cand, cand), :] = qb[
                t, :, h * HD : (h + 1) * HD
            ].astype(jnp.float32)
    for which, source in enumerate((nkb, nvb)):
        for t in range(steps):
            nf[which, pl.ds(t * cand, cand), :] = source[t].astype(jnp.float32)
        nf[which, pl.ds(steps * cand, (8 - steps) * cand), :] = jnp.zeros(
            ((8 - steps) * cand, HD), jnp.float32
        )
    empty = jnp.zeros((PAD - 8, HD), jnp.float32)
    for c in range(cand):
        for which, target in enumerate((kx, vx)):
            rows = nf[which, pl.ds(c, 8, stride=cand), :]
            target[c, pl.ds(cache, PAD), :] = jnp.concatenate([rows, empty], axis=0).astype(
                jnp.bfloat16
            )
    for copy in ins[3:]:
        copy.wait()

    width = cache + PAD
    lane = lax.broadcasted_iota(jnp.int32, (2 * heads, width), 1)
    step_of_row = lax.broadcasted_iota(jnp.int32, (2 * heads, width), 0) // heads
    rate = math.log2(math.e) / math.sqrt(HD)

    def attend(cands, first_step):
        fresh_seen = (lane >= cache) & (lane <= cache + first_step + step_of_row)
        scores = []
        for c in cands:
            q = jnp.concatenate(
                [
                    qf[pl.ds((first_step + i) * heads * cand + c, heads, stride=cand), :]
                    for i in range(2)
                ],
                axis=0,
            ).astype(jnp.bfloat16)
            s = lax.dot_general(q, kx[c], NT, preferred_element_type=jnp.float32)
            scores.append(jnp.where((lane < lengths_s[c]) | fresh_seen, s, NEG))
        tops = [jnp.max(s, axis=1, keepdims=True) for s in scores]
        weights = [jnp.exp2((s - m) * rate) for s, m in zip(scores, tops)]
        totals = [jnp.sum(w, axis=1, keepdims=True) for w in weights]
        return [
            jnp.dot(w.astype(jnp.bfloat16), vx[c], preferred_element_type=jnp.float32)
            / total
            for c, w, total in zip(cands, weights, totals)
        ]

    def late_block(b, _):
        cands = [kept_s[0, b * BLOCK + j] for j in range(BLOCK)]
        outs = attend(cands, steps // 2)
        for j, o in enumerate(outs):
            late_buf[b * BLOCK + j] = o.astype(jnp.bfloat16)
        return 0

    late_buf[kept_n] = jnp.zeros(late_buf.shape[1:], jnp.bfloat16)
    lax.fori_loop(0, kept_n // BLOCK, late_block, 0)

    for sem in (my_send, my_recv):
        all_of(meta_y, yn - 1, sem).wait()
    meta_all[z_me] = jnp.sum(meta_y[...], axis=0)

    def z_copy(d):
        return pltpu.make_async_remote_copy(
            src_ref=meta_all.at[z_me],
            dst_ref=meta_all.at[z_me],
            send_sem=mz_send,
            recv_sem=mz_recv,
            device_id=(lax.rem(z_me + d, zn) * yn + y_me, t_me),
            device_id_type=MESH,
        )

    lax.fori_loop(1, zn, lambda d, _: (z_copy(d).start(), 0)[1], 0)

    to_smem.wait()
    for g in range(groups):
        send[g] = late_buf[idx_s[0, 0, g]]

    def row_copy(d):
        g = lax.rem(g_me + d, groups)
        return pltpu.make_async_remote_copy(
            src_ref=send.at[g],
            dst_ref=recv.at[g_me],
            send_sem=send_sem,
            recv_sem=recv_sem,
            device_id=(g, t_me),
            device_id_type=MESH,
        )

    lax.fori_loop(1, groups, lambda d, _: (row_copy(d).start(), 0)[1], 0)
    recv[g_me] = send[g_me]

    def early_block(b, _):
        cands = [b * BLOCK + j for j in range(BLOCK)]
        outs = attend(cands, 0)
        for c, o in zip(cands, outs):
            for i in range(2):
                of[pl.ds(i * heads * cand + c, heads, stride=cand), :] = o[
                    i * heads : (i + 1) * heads
                ]
        return 0

    lax.fori_loop(0, cand // BLOCK, early_block, 0)
    for t in range(2):
        for h in range(heads):
            stage[t, :, h * HD : (h + 1) * HD] = of[
                pl.ds((t * heads + h) * cand, cand), :
            ].astype(jnp.bfloat16)
    early_copy = pltpu.make_async_copy(stage, early_h, out_sem.at[0])
    early_copy.start()
    rw[t_me] = jnp.zeros(rw.shape[1:], jnp.float32)
    rw[t_me, :, pl.ds(0, cand)] = lax.dot_general(
        weight_v[...], stage[1], NT, preferred_element_type=jnp.float32
    )

    def rw_copy(d):
        return pltpu.make_async_remote_copy(
            src_ref=rw.at[t_me],
            dst_ref=rw.at[t_me],
            send_sem=rw_send,
            recv_sem=rw_recv,
            device_id=(g_me, lax.rem(t_me + d, tn)),
            device_id_type=MESH,
        )

    lax.fori_loop(1, tn, lambda d, _: (rw_copy(d).start(), 0)[1], 0)

    if zn > 1:
        for sem in (mz_send, mz_recv):
            all_of(meta_all, zn - 1, sem).wait()
    met = meta_all[...].reshape(zn * RING, 128)
    lane_m = lax.broadcasted_iota(jnp.int32, (zn * RING, 128), 1)
    sub_m = lax.broadcasted_iota(jnp.int32, (zn * RING, 128), 0)
    slots_here = jnp.sum(jnp.where(lane_m == g_me, met, 0), axis=1, keepdims=True)
    sender = (sub_m // RING) * yn + sub_m % RING
    row_v[1] = jnp.max(
        jnp.where(slots_here == lane_m + 1, sender, 0), axis=0, keepdims=True
    )
    back = pltpu.make_async_copy(row_v.at[1], idx_s.at[1], row_sem.at[1])
    back.start()
    back.wait()

    for sem in (send_sem, recv_sem):
        all_of(recv, groups - 1, sem).wait()
    for p in range(kept_n):
        o = recv[idx_s[1, 0, p]].astype(jnp.float32)
        for i in range(2):
            of[pl.ds(i * heads * kept_n + p, heads, stride=kept_n), :] = o[
                i * heads : (i + 1) * heads
            ]
    for t in range(2):
        for h in range(heads):
            late_stage[t, :, h * HD : (h + 1) * HD] = of[
                pl.ds((t * heads + h) * kept_n, kept_n), :
            ].astype(jnp.bfloat16)
    late_copy = pltpu.make_async_copy(late_stage, late_h, out_sem.at[1])
    late_copy.start()
    if tn > 1:
        for sem in (rw_send, rw_recv):
            all_of(rw, tn - 1, sem).wait()
    reward_o[...] = jnp.sum(rw[...], axis=0)[:, :cand]
    early_copy.wait()
    late_copy.wait()


def local(
    ring,
    tn,
    cache_keys,
    cache_values,
    lengths,
    queries,
    new_keys,
    new_values,
    reward_weight,
    kept_candidates,
    arrival_cohort,
    arrival_place,
):
    zn, yn = ring
    groups = zn * yn
    cand, cache, _ = cache_keys.shape
    steps, _, columns = queries.shape
    heads = columns // HD
    kept_n = kept_candidates.shape[1]
    half = steps // 2
    bf16, f32, i32 = jnp.bfloat16, jnp.float32, jnp.int32
    smem = pl.BlockSpec(memory_space=pltpu.SMEM)
    vmem = pl.BlockSpec(memory_space=pltpu.VMEM)
    hbm = pl.BlockSpec(memory_space=pl.ANY)
    dma = pltpu.SemaphoreType.DMA
    early, reward, late = pl.pallas_call(
        functools.partial(kernel, (zn, yn, tn, cand, kept_n, heads)),
        out_shape=(
            jax.ShapeDtypeStruct((half, cand, columns), bf16),
            jax.ShapeDtypeStruct((1, cand), f32),
            jax.ShapeDtypeStruct((half, kept_n, columns), bf16),
        ),
        in_specs=[smem, smem, vmem, vmem, vmem, hbm, hbm, hbm, hbm, hbm],
        out_specs=(hbm, vmem, hbm),
        scratch_shapes=[
            pltpu.VMEM((cand, cache + PAD, HD), bf16),
            pltpu.VMEM((cand, cache + PAD, HD), bf16),
            pltpu.VMEM(queries.shape, bf16),
            pltpu.VMEM(new_keys.shape, bf16),
            pltpu.VMEM(new_values.shape, bf16),
            pltpu.VMEM((steps * heads * cand, HD), f32),
            pltpu.VMEM((2, 8 * cand, HD), f32),
            pltpu.VMEM((half * heads * cand, HD), f32),
            pltpu.VMEM((kept_n + 1, half * heads, HD), bf16),
            pltpu.VMEM((groups, half * heads, HD), bf16),
            pltpu.VMEM((groups, half * heads, HD), bf16),
            pltpu.VMEM((half, cand, columns), bf16),
            pltpu.VMEM((half, kept_n, columns), bf16),
            pltpu.VMEM((2, 1, 128), i32),
            pltpu.SMEM((2, 1, 128), i32),
            pltpu.VMEM((RING, 128), i32),
            pltpu.VMEM((yn, RING, 128), i32),
            pltpu.VMEM((zn, RING, 128), i32),
            pltpu.VMEM((tn, 1, 128), f32),
            dma((5,)), dma((2,)), dma((2,)),
            dma, dma, dma, dma, dma, dma, dma, dma,
        ],
        compiler_params=pltpu.CompilerParams(
            collective_id=0, has_side_effects=True, vmem_limit_bytes=60 * 1024 * 1024
        ),
    )(
        kept_candidates,
        lengths,
        arrival_cohort,
        arrival_place,
        reward_weight.reshape(1, columns),
        cache_keys,
        cache_values,
        queries,
        new_keys,
        new_values,
    )
    return early, reward.reshape(cand), late


def solution(mesh):
    groups, tn = mesh.shape["dp"], mesh.shape["tensor"]
    yn = min(RING, groups)
    placed = (
        P("dp", None, "tensor"),
        P("dp", None, "tensor"),
        P("dp"),
        P(None, "dp", "tensor"),
        P(None, "dp", "tensor"),
        P(None, "dp", "tensor"),
        P("tensor"),
        P("dp", None),
        P("dp", None),
        P("dp", None),
    )
    return jax.shard_map(
        functools.partial(local, (groups // yn, yn), tn),
        mesh=mesh,
        in_specs=placed,
        out_specs=(P(None, "dp", "tensor"), P("dp"), P(None, "dp", "tensor")),
        check_vma=False,
    )
```

```python
import functools
import math

import jax
import jax.numpy as jnp
from jax import lax
from jax.experimental import pallas as pl
from jax.experimental.pallas import tpu as pltpu
from jax.sharding import PartitionSpec as P

MESH = pl.DeviceIdType.MESH
HD = 128
PAD = 16
BLOCK = 8
RING = 8
NEG = -1e30
NT = (((1,), (1,)), ((), ()))


def all_of(ref, count, sem):
    part = ref.at[pl.ds(0, count)]
    return pltpu.make_async_copy(part, part, sem)


def kernel(
    dims,
    kept_h, lengths_h, cohort_h, place_h, weight_h,
    keys_h, values_h, queries_h, fresh_k_h, fresh_v_h,
    stage, reward_o, late_stage,
    kept_s, lengths_s, cohort_v, place_v, weight_v,
    kx, vx, qb, nkb, nvb, qf, nf, of, late_buf, send, recv,
    row_v, idx_s, meta_mine, meta_all, rw,
    in_sem, row_sem, send_sem, recv_sem, meta_send, meta_recv, rw_send, rw_recv,
):
    zn, yn, tn, cand, kept_n, heads = dims
    groups = zn * yn
    cache = kx.shape[1] - PAD
    g_me = lax.axis_index("dp")
    t_me = lax.axis_index("tensor")
    z_me, y_me = g_me // yn, g_me % yn

    def hops(offset):
        return min(offset[0], zn - offset[0]) + min(offset[1], yn - offset[1])

    others = sorted(((i, j) for i in range(zn) for j in range(yn)), key=hops)[:0:-1]
    others = [
        lax.rem(z_me + i, zn) * yn + lax.rem(y_me + j, yn) for i, j in others
    ]

    ins = [
        pltpu.make_async_copy(src, dst, in_sem.at[i])
        for i, (src, dst) in enumerate(
            (
                (cohort_h, cohort_v),
                (place_h, place_v),
                (fresh_k_h, nkb),
                (fresh_v_h, nvb),
                (queries_h, qb),
                (kept_h, kept_s),
                (lengths_h, lengths_s),
                (keys_h, kx.at[:, pl.ds(0, cache), :]),
                (values_h, vx.at[:, pl.ds(0, cache), :]),
                (weight_h, weight_v),
            )
        )
    ]
    for copy in ins:
        copy.start()

    barrier = pltpu.get_barrier_semaphore()

    for g in others:
        pl.semaphore_signal(barrier, inc=1, device_id=(g, t_me), device_id_type=MESH)

    def greet_t(d, _):
        pl.semaphore_signal(
            barrier, inc=1, device_id=(g_me, lax.rem(t_me + d, tn)), device_id_type=MESH
        )
        return 0

    lax.fori_loop(1, tn, greet_t, 0)

    for copy in ins[:2]:
        copy.wait()

    eye = lax.broadcasted_iota(jnp.int32, (kept_n, kept_n), 0) == lax.broadcasted_iota(
        jnp.int32, (kept_n, kept_n), 1
    )

    def column(row):
        return jnp.sum(jnp.where(eye, row, 0), axis=1, keepdims=True)

    lane_g = lax.broadcasted_iota(jnp.int32, (kept_n, 128), 1)
    sub_k = lax.broadcasted_iota(jnp.int32, (kept_n, 128), 0)
    hit = column(cohort_v[...]) == lane_g
    chosen = jnp.min(jnp.where(hit, sub_k, kept_n), axis=0, keepdims=True)
    row_v[0] = chosen
    to_smem = pltpu.make_async_copy(row_v.at[0], idx_s.at[0], row_sem.at[0])
    to_smem.start()
    slot_of = jnp.max(
        jnp.where(
            cohort_v[...] == lax.broadcasted_iota(jnp.int32, (groups, kept_n), 0),
            place_v[...] + 1,
            0,
        ),
        axis=1,
        keepdims=True,
    )
    meta_mine[...] = jnp.broadcast_to(slot_of, (groups, 128)).reshape(groups, 1, 128)

    for copy in ins[2:5]:
        copy.wait()
    steps = qb.shape[0]

    def spread_queries(which):
        for t in which:
            for h in range(heads):
                qf[pl.ds((t * heads + h) * cand, cand), :] = qb[
                    t, :, h * HD : (h + 1) * HD
                ].astype(jnp.float32)

    spread_queries(range(steps // 2, steps))
    for which, source in enumerate((nkb, nvb)):
        for t in range(steps):
            nf[which, pl.ds(t * cand, cand), :] = source[t].astype(jnp.float32)
        nf[which, pl.ds(steps * cand, (8 - steps) * cand), :] = jnp.zeros(
            ((8 - steps) * cand, HD), jnp.float32
        )
    empty = jnp.zeros((PAD - 8, HD), jnp.float32)
    for c in range(cand):
        for which, target in enumerate((kx, vx)):
            rows = nf[which, pl.ds(c, 8, stride=cand), :]
            target[c, pl.ds(cache, PAD), :] = jnp.concatenate([rows, empty], axis=0).astype(
                jnp.bfloat16
            )
    for copy in ins[5:]:
        copy.wait()

    width = cache + PAD
    lane = lax.broadcasted_iota(jnp.int32, (2 * heads, width), 1)
    step_of_row = lax.broadcasted_iota(jnp.int32, (2 * heads, width), 0) // heads
    rate = math.log2(math.e) / math.sqrt(HD)

    def attend(cands, first_step):
        fresh_seen = (lane >= cache) & (lane <= cache + first_step + step_of_row)
        scores = []
        for c in cands:
            q = jnp.concatenate(
                [
                    qf[pl.ds((first_step + i) * heads * cand + c, heads, stride=cand), :]
                    for i in range(2)
                ],
                axis=0,
            ).astype(jnp.bfloat16)
            s = lax.dot_general(q, kx[c], NT, preferred_element_type=jnp.float32)
            scores.append(jnp.where((lane < lengths_s[c]) | fresh_seen, s, NEG))
        tops = [jnp.max(s, axis=1, keepdims=True) for s in scores]
        weights = [jnp.exp2((s - m) * rate) for s, m in zip(scores, tops)]
        totals = [jnp.sum(w, axis=1, keepdims=True) for w in weights]
        return [
            jnp.dot(w.astype(jnp.bfloat16), vx[c], preferred_element_type=jnp.float32)
            / total
            for c, w, total in zip(cands, weights, totals)
        ]

    def late_block(b, _):
        cands = [kept_s[0, b * BLOCK + j] for j in range(BLOCK)]
        outs = attend(cands, steps // 2)
        for j, o in enumerate(outs):
            late_buf[b * BLOCK + j] = o.astype(jnp.bfloat16)
        return 0

    late_buf[kept_n] = jnp.zeros(late_buf.shape[1:], jnp.bfloat16)
    lax.fori_loop(0, kept_n // BLOCK, late_block, 0)

    to_smem.wait()
    for g in range(groups):
        send[g] = late_buf[idx_s[0, 0, g]]

    pl.semaphore_wait(barrier, groups - 1 + tn - 1)
    for g in others:
        pltpu.make_async_remote_copy(
            src_ref=meta_mine.at[g],
            dst_ref=meta_all.at[g_me],
            send_sem=meta_send,
            recv_sem=meta_recv,
            device_id=(g, t_me),
            device_id_type=MESH,
        ).start()
    for g in others:
        pltpu.make_async_remote_copy(
            src_ref=send.at[g],
            dst_ref=recv.at[g_me],
            send_sem=send_sem,
            recv_sem=recv_sem,
            device_id=(g, t_me),
            device_id_type=MESH,
        ).start()
    meta_all[g_me] = meta_mine[g_me]
    recv[g_me] = send[g_me]

    spread_queries(range(steps // 2))

    def early_block(b, _):
        cands = [b * BLOCK + j for j in range(BLOCK)]
        outs = attend(cands, 0)
        for c, o in zip(cands, outs):
            for i in range(2):
                of[pl.ds(i * heads * cand + c, heads, stride=cand), :] = o[
                    i * heads : (i + 1) * heads
                ]
        return 0

    lax.fori_loop(0, cand // BLOCK, early_block, 0)
    for t in range(2):
        for h in range(heads):
            stage[t, :, h * HD : (h + 1) * HD] = of[
                pl.ds((t * heads + h) * cand, cand), :
            ].astype(jnp.bfloat16)
    rw[t_me] = jnp.zeros(rw.shape[1:], jnp.float32)
    rw[t_me, :, pl.ds(0, cand)] = lax.dot_general(
        weight_v[...].reshape(1, heads * HD), stage[1], NT, preferred_element_type=jnp.float32
    )

    def rw_copy(d):
        return pltpu.make_async_remote_copy(
            src_ref=rw.at[t_me],
            dst_ref=rw.at[t_me],
            send_sem=rw_send,
            recv_sem=rw_recv,
            device_id=(g_me, lax.rem(t_me + d, tn)),
            device_id_type=MESH,
        )

    lax.fori_loop(1, tn, lambda d, _: (rw_copy(d).start(), 0)[1], 0)

    for sem in (meta_send, meta_recv):
        all_of(meta_all, groups - 1, sem).wait()
    slots_here = meta_all[...].reshape(groups, 128)
    lane_m = lax.broadcasted_iota(jnp.int32, (groups, 128), 1)
    sender = lax.broadcasted_iota(jnp.int32, (groups, 128), 0)
    row_v[1] = jnp.max(
        jnp.where(slots_here == lane_m + 1, sender, 0), axis=0, keepdims=True
    )
    back = pltpu.make_async_copy(row_v.at[1], idx_s.at[1], row_sem.at[1])
    back.start()
    back.wait()

    for sem in (send_sem, recv_sem):
        all_of(recv, groups - 1, sem).wait()
    for p in range(kept_n):
        o = recv[idx_s[1, 0, p]].astype(jnp.float32)
        for i in range(2):
            of[pl.ds(i * heads * kept_n + p, heads, stride=kept_n), :] = o[
                i * heads : (i + 1) * heads
            ]
    for t in range(2):
        for h in range(heads):
            late_stage[t, :, h * HD : (h + 1) * HD] = of[
                pl.ds((t * heads + h) * kept_n, kept_n), :
            ].astype(jnp.bfloat16)
    if tn > 1:
        for sem in (rw_send, rw_recv):
            all_of(rw, tn - 1, sem).wait()
    reward_o[...] = jnp.sum(rw[...], axis=0)[:, :cand]


def write_out(early_v, reward_v, late_v, early_h, reward_h, late_h, sems):
    copies = [
        pltpu.make_async_copy(src, dst, sems.at[i])
        for i, (src, dst) in enumerate(
            ((early_v, early_h), (late_v, late_h), (reward_v, reward_h))
        )
    ]
    for copy in copies:
        copy.start()
    for copy in copies:
        copy.wait()


def local(
    ring,
    tn,
    cache_keys,
    cache_values,
    lengths,
    queries,
    new_keys,
    new_values,
    reward_weight,
    kept_candidates,
    arrival_cohort,
    arrival_place,
):
    zn, yn = ring
    groups = zn * yn
    cand, cache, _ = cache_keys.shape
    steps, _, columns = queries.shape
    heads = columns // HD
    kept_n = kept_candidates.shape[1]
    half = steps // 2
    bf16, f32, i32 = jnp.bfloat16, jnp.float32, jnp.int32
    anywhere = pl.BlockSpec(memory_space=pl.ANY)
    dma = pltpu.SemaphoreType.DMA
    shapes = (
        ((half, cand, columns), bf16),
        ((1, cand), f32),
        ((half, kept_n, columns), bf16),
    )
    in_hbm = [
        pltpu.with_memory_space_constraint(x, pltpu.HBM)
        for x in (
            kept_candidates,
            lengths,
            arrival_cohort,
            arrival_place,
            reward_weight,
            cache_keys,
            cache_values,
            queries,
            new_keys,
            new_values,
        )
    ]
    staged = pl.pallas_call(
        functools.partial(kernel, (zn, yn, tn, cand, kept_n, heads)),
        out_shape=tuple(pltpu.VMEM(*shape) for shape in shapes),
        in_specs=[anywhere] * len(in_hbm),
        out_specs=(pl.BlockSpec(memory_space=pltpu.VMEM),) * 3,
        scratch_shapes=[
            pltpu.SMEM(kept_candidates.shape, i32),
            pltpu.SMEM(lengths.shape, i32),
            pltpu.VMEM(arrival_cohort.shape, i32),
            pltpu.VMEM(arrival_place.shape, i32),
            pltpu.VMEM(reward_weight.shape, bf16),
            pltpu.VMEM((cand, cache + PAD, HD), bf16),
            pltpu.VMEM((cand, cache + PAD, HD), bf16),
            pltpu.VMEM(queries.shape, bf16),
            pltpu.VMEM(new_keys.shape, bf16),
            pltpu.VMEM(new_values.shape, bf16),
            pltpu.VMEM((steps * heads * cand, HD), f32),
            pltpu.VMEM((2, 8 * cand, HD), f32),
            pltpu.VMEM((half * heads * cand, HD), f32),
            pltpu.VMEM((kept_n + 1, half * heads, HD), bf16),
            pltpu.VMEM((groups, half * heads, HD), bf16),
            pltpu.VMEM((groups, half * heads, HD), bf16),
            pltpu.VMEM((2, 1, 128), i32),
            pltpu.SMEM((2, 1, 128), i32),
            pltpu.VMEM((groups, 1, 128), i32),
            pltpu.VMEM((groups, 1, 128), i32),
            pltpu.VMEM((tn, 1, 128), f32),
            dma((len(in_hbm),)), dma((2,)),
            dma, dma, dma, dma, dma, dma,
        ],
        compiler_params=pltpu.CompilerParams(
            collective_id=0, has_side_effects=True, vmem_limit_bytes=40 * 1024 * 1024
        ),
    )(*in_hbm)
    early, reward, late = pl.pallas_call(
        write_out,
        out_shape=tuple(pltpu.HBM(*shape) for shape in shapes),
        in_specs=[anywhere] * 3,
        out_specs=(anywhere,) * 3,
        scratch_shapes=[dma((3,))],
        compiler_params=pltpu.CompilerParams(vmem_limit_bytes=2 * 1024 * 1024),
    )(*(pltpu.with_memory_space_constraint(x, pltpu.VMEM) for x in staged))
    return early, reward.reshape(cand), late


def solution(mesh):
    groups, tn = mesh.shape["dp"], mesh.shape["tensor"]
    yn = min(RING, groups)
    placed = (
        P("dp", None, "tensor"),
        P("dp", None, "tensor"),
        P("dp"),
        P(None, "dp", "tensor"),
        P(None, "dp", "tensor"),
        P(None, "dp", "tensor"),
        P("tensor"),
        P("dp", None),
        P("dp", None),
        P("dp", None),
    )
    return jax.shard_map(
        functools.partial(local, (groups // yn, yn), tn),
        mesh=mesh,
        in_specs=placed,
        out_specs=(P(None, "dp", "tensor"), P("dp"), P(None, "dp", "tensor")),
        check_vma=False,
    )
```

```python
import functools
import math

import jax
import jax.numpy as jnp
from jax import lax
from jax.experimental import pallas as pl
from jax.experimental.pallas import tpu as pltpu
from jax.sharding import PartitionSpec as P

MESH = pl.DeviceIdType.MESH
HD = 128
PAD = 16
BLOCK = 8
RING = 8
NEG = -1e30
NT = (((1,), (1,)), ((), ()))


def all_of(ref, count, sem):
    part = ref.at[pl.ds(0, count)]
    return pltpu.make_async_copy(part, part, sem)


def kernel(
    dims,
    kept_h, lengths_h, cohort_h, place_h, weight_h,
    keys_h, values_h, queries_h, fresh_k_h, fresh_v_h,
    stage, reward_o, late_stage,
    kept_s, lengths_s, cohort_v, place_v, weight_v,
    kx, vx, qb, nkb, nvb, qf, nf, of, late_buf, send, recv,
    row_v, idx_s, meta_mine, meta_all, rw,
    in_sem, row_sem, send_sem, recv_sem, meta_send, meta_recv, rw_send, rw_recv,
    ready_sem,
):
    zn, yn, tn, cand, kept_n, heads = dims
    groups = zn * yn
    cache = kx.shape[1] - PAD
    g_me = lax.axis_index("dp")
    t_me = lax.axis_index("tensor")
    z_me, y_me = g_me // yn, g_me % yn

    ins = [
        pltpu.make_async_copy(src, dst, in_sem.at[i])
        for i, (src, dst) in enumerate(
            (
                (cohort_h, cohort_v),
                (place_h, place_v),
                (fresh_k_h, nkb),
                (fresh_v_h, nvb),
                (queries_h, qb),
                (kept_h, kept_s),
                (lengths_h, lengths_s),
                (keys_h, kx.at[:, pl.ds(0, cache), :]),
                (values_h, vx.at[:, pl.ds(0, cache), :]),
                (weight_h, weight_v),
            )
        )
    ]
    for copy in ins:
        copy.start()

    barrier = pltpu.get_barrier_semaphore()

    def greet(g, _):
        pl.semaphore_signal(barrier, inc=1, device_id=(g, t_me), device_id_type=MESH)
        return 0

    lax.fori_loop(g_me + 1, groups, greet, 0)

    def greet_t(d, _):
        pl.semaphore_signal(
            barrier, inc=1, device_id=(g_me, lax.rem(t_me + d, tn)), device_id_type=MESH
        )
        return 0

    lax.fori_loop(1, tn, greet_t, 0)

    for copy in ins[:2]:
        copy.wait()

    eye = lax.broadcasted_iota(jnp.int32, (kept_n, kept_n), 0) == lax.broadcasted_iota(
        jnp.int32, (kept_n, kept_n), 1
    )

    def column(row):
        return jnp.sum(jnp.where(eye, row, 0), axis=1, keepdims=True)

    lane_g = lax.broadcasted_iota(jnp.int32, (kept_n, 128), 1)
    sub_k = lax.broadcasted_iota(jnp.int32, (kept_n, 128), 0)
    hit = column(cohort_v[...]) == lane_g
    chosen = jnp.min(jnp.where(hit, sub_k, kept_n), axis=0, keepdims=True)
    row_v[0] = chosen
    to_smem = pltpu.make_async_copy(row_v.at[0], idx_s.at[0], row_sem.at[0])
    to_smem.start()
    slot_of = jnp.max(
        jnp.where(
            cohort_v[...] == lax.broadcasted_iota(jnp.int32, (groups, kept_n), 0),
            place_v[...] + 1,
            0,
        ),
        axis=1,
        keepdims=True,
    )
    meta_mine[...] = jnp.broadcast_to(slot_of, (groups, 128)).reshape(groups, 1, 128)

    for copy in ins[2:5]:
        copy.wait()
    steps = qb.shape[0]

    def spread_queries(which):
        for t in which:
            for h in range(heads):
                qf[pl.ds((t * heads + h) * cand, cand), :] = qb[
                    t, :, h * HD : (h + 1) * HD
                ].astype(jnp.float32)

    spread_queries(range(steps // 2, steps))
    for which, source in enumerate((nkb, nvb)):
        for t in range(steps):
            nf[which, pl.ds(t * cand, cand), :] = source[t].astype(jnp.float32)
        nf[which, pl.ds(steps * cand, (8 - steps) * cand), :] = jnp.zeros(
            ((8 - steps) * cand, HD), jnp.float32
        )
    empty = jnp.zeros((PAD - 8, HD), jnp.float32)
    for c in range(cand):
        for which, target in enumerate((kx, vx)):
            rows = nf[which, pl.ds(c, 8, stride=cand), :]
            target[c, pl.ds(cache, PAD), :] = jnp.concatenate([rows, empty], axis=0).astype(
                jnp.bfloat16
            )
    for copy in ins[5:]:
        copy.wait()

    width = cache + PAD
    lane = lax.broadcasted_iota(jnp.int32, (2 * heads, width), 1)
    step_of_row = lax.broadcasted_iota(jnp.int32, (2 * heads, width), 0) // heads
    rate = math.log2(math.e) / math.sqrt(HD)

    def attend(cands, first_step):
        fresh_seen = (lane >= cache) & (lane <= cache + first_step + step_of_row)
        scores = []
        for c in cands:
            q = jnp.concatenate(
                [
                    qf[pl.ds((first_step + i) * heads * cand + c, heads, stride=cand), :]
                    for i in range(2)
                ],
                axis=0,
            ).astype(jnp.bfloat16)
            s = lax.dot_general(q, kx[c], NT, preferred_element_type=jnp.float32)
            scores.append(jnp.where((lane < lengths_s[c]) | fresh_seen, s, NEG))
        tops = [jnp.max(s, axis=1, keepdims=True) for s in scores]
        weights = [jnp.exp2((s - m) * rate) for s, m in zip(scores, tops)]
        totals = [jnp.sum(w, axis=1, keepdims=True) for w in weights]
        return [
            jnp.dot(w.astype(jnp.bfloat16), vx[c], preferred_element_type=jnp.float32)
            / total
            for c, w, total in zip(cands, weights, totals)
        ]

    def late_block(b, _):
        cands = [kept_s[0, b * BLOCK + j] for j in range(BLOCK)]
        outs = attend(cands, steps // 2)
        for j, o in enumerate(outs):
            late_buf[b * BLOCK + j] = o.astype(jnp.bfloat16)
        return 0

    late_buf[kept_n] = jnp.zeros(late_buf.shape[1:], jnp.bfloat16)
    lax.fori_loop(0, kept_n // BLOCK, late_block, 0)

    to_smem.wait()
    for g in range(groups):
        send[g] = late_buf[idx_s[0, 0, g]]

    def send_to(g, _):
        for src, dst, sem_here, sem_there in (
            (meta_mine, meta_all, meta_send, meta_recv),
            (send, recv, send_sem, recv_sem),
        ):
            pltpu.make_async_remote_copy(
                src_ref=src.at[g],
                dst_ref=dst.at[g_me],
                send_sem=sem_here,
                recv_sem=sem_there,
                device_id=(g, t_me),
                device_id_type=MESH,
            ).start()
        return 0

    def tell(g, _):
        pl.semaphore_signal(
            ready_sem.at[z_me], inc=1, device_id=(g, t_me), device_id_type=MESH
        )
        return 0

    if tn > 1:
        pl.semaphore_wait(barrier, g_me + tn - 1)
    else:

        @pl.when(g_me > 0)
        def _():
            pl.semaphore_wait(barrier, g_me)

    lax.fori_loop(0, g_me, send_to, 0)
    lax.fori_loop(0, g_me, tell, 0)
    meta_all[g_me] = meta_mine[g_me]
    recv[g_me] = send[g_me]

    spread_queries(range(steps // 2))

    def early_block(b, _):
        cands = [b * BLOCK + j for j in range(BLOCK)]
        outs = attend(cands, 0)
        for c, o in zip(cands, outs):
            for i in range(2):
                of[pl.ds(i * heads * cand + c, heads, stride=cand), :] = o[
                    i * heads : (i + 1) * heads
                ]
        return 0

    lax.fori_loop(0, cand // BLOCK, early_block, 0)
    for t in range(2):
        for h in range(heads):
            stage[t, :, h * HD : (h + 1) * HD] = of[
                pl.ds((t * heads + h) * cand, cand), :
            ].astype(jnp.bfloat16)
    rw[t_me] = jnp.zeros(rw.shape[1:], jnp.float32)
    rw[t_me, :, pl.ds(0, cand)] = lax.dot_general(
        weight_v[...].reshape(1, heads * HD), stage[1], NT, preferred_element_type=jnp.float32
    )

    def rw_copy(d):
        return pltpu.make_async_remote_copy(
            src_ref=rw.at[t_me],
            dst_ref=rw.at[t_me],
            send_sem=rw_send,
            recv_sem=rw_recv,
            device_id=(g_me, lax.rem(t_me + d, tn)),
            device_id_type=MESH,
        )

    lax.fori_loop(1, tn, lambda d, _: (rw_copy(d).start(), 0)[1], 0)

    @pl.when(y_me < yn - 1)
    def _():
        pl.semaphore_wait(ready_sem.at[z_me], yn - 1 - y_me)
        lax.fori_loop(g_me + 1, (z_me + 1) * yn, send_to, 0)

    def later_plane(z, _):
        pl.semaphore_wait(ready_sem.at[z], yn)
        for y in range(yn):
            send_to(z * yn + y, 0)
        return 0

    lax.fori_loop(z_me + 1, zn, later_plane, 0)

    for sem in (meta_send, meta_recv):
        all_of(meta_all, groups - 1, sem).wait()
    slots_here = meta_all[...].reshape(groups, 128)
    lane_m = lax.broadcasted_iota(jnp.int32, (groups, 128), 1)
    sender = lax.broadcasted_iota(jnp.int32, (groups, 128), 0)
    row_v[1] = jnp.max(
        jnp.where(slots_here == lane_m + 1, sender, 0), axis=0, keepdims=True
    )
    back = pltpu.make_async_copy(row_v.at[1], idx_s.at[1], row_sem.at[1])
    back.start()
    back.wait()

    for sem in (send_sem, recv_sem):
        all_of(recv, groups - 1, sem).wait()
    for p in range(kept_n):
        o = recv[idx_s[1, 0, p]].astype(jnp.float32)
        for i in range(2):
            of[pl.ds(i * heads * kept_n + p, heads, stride=kept_n), :] = o[
                i * heads : (i + 1) * heads
            ]
    for t in range(2):
        for h in range(heads):
            late_stage[t, :, h * HD : (h + 1) * HD] = of[
                pl.ds((t * heads + h) * kept_n, kept_n), :
            ].astype(jnp.bfloat16)
    if tn > 1:
        for sem in (rw_send, rw_recv):
            all_of(rw, tn - 1, sem).wait()
    reward_o[...] = jnp.sum(rw[...], axis=0)[:, :cand]


def write_out(early_v, reward_v, late_v, early_h, reward_h, late_h, sems):
    copies = [
        pltpu.make_async_copy(src, dst, sems.at[i])
        for i, (src, dst) in enumerate(
            ((early_v, early_h), (late_v, late_h), (reward_v, reward_h))
        )
    ]
    for copy in copies:
        copy.start()
    for copy in copies:
        copy.wait()


def local(
    ring,
    tn,
    cache_keys,
    cache_values,
    lengths,
    queries,
    new_keys,
    new_values,
    reward_weight,
    kept_candidates,
    arrival_cohort,
    arrival_place,
):
    zn, yn = ring
    groups = zn * yn
    cand, cache, _ = cache_keys.shape
    steps, _, columns = queries.shape
    heads = columns // HD
    kept_n = kept_candidates.shape[1]
    half = steps // 2
    bf16, f32, i32 = jnp.bfloat16, jnp.float32, jnp.int32
    anywhere = pl.BlockSpec(memory_space=pl.ANY)
    dma = pltpu.SemaphoreType.DMA
    shapes = (
        ((half, cand, columns), bf16),
        ((1, cand), f32),
        ((half, kept_n, columns), bf16),
    )
    in_hbm = [
        pltpu.with_memory_space_constraint(x, pltpu.HBM)
        for x in (
            kept_candidates,
            lengths,
            arrival_cohort,
            arrival_place,
            reward_weight,
            cache_keys,
            cache_values,
            queries,
            new_keys,
            new_values,
        )
    ]
    staged = pl.pallas_call(
        functools.partial(kernel, (zn, yn, tn, cand, kept_n, heads)),
        out_shape=tuple(pltpu.VMEM(*shape) for shape in shapes),
        in_specs=[anywhere] * len(in_hbm),
        out_specs=(pl.BlockSpec(memory_space=pltpu.VMEM),) * 3,
        scratch_shapes=[
            pltpu.SMEM(kept_candidates.shape, i32),
            pltpu.SMEM(lengths.shape, i32),
            pltpu.VMEM(arrival_cohort.shape, i32),
            pltpu.VMEM(arrival_place.shape, i32),
            pltpu.VMEM(reward_weight.shape, bf16),
            pltpu.VMEM((cand, cache + PAD, HD), bf16),
            pltpu.VMEM((cand, cache + PAD, HD), bf16),
            pltpu.VMEM(queries.shape, bf16),
            pltpu.VMEM(new_keys.shape, bf16),
            pltpu.VMEM(new_values.shape, bf16),
            pltpu.VMEM((steps * heads * cand, HD), f32),
            pltpu.VMEM((2, 8 * cand, HD), f32),
            pltpu.VMEM((half * heads * cand, HD), f32),
            pltpu.VMEM((kept_n + 1, half * heads, HD), bf16),
            pltpu.VMEM((groups, half * heads, HD), bf16),
            pltpu.VMEM((groups, half * heads, HD), bf16),
            pltpu.VMEM((2, 1, 128), i32),
            pltpu.SMEM((2, 1, 128), i32),
            pltpu.VMEM((groups, 1, 128), i32),
            pltpu.VMEM((groups, 1, 128), i32),
            pltpu.VMEM((tn, 1, 128), f32),
            dma((len(in_hbm),)), dma((2,)),
            dma, dma, dma, dma, dma, dma,
            pltpu.SemaphoreType.REGULAR((zn,)),
        ],
        compiler_params=pltpu.CompilerParams(
            collective_id=0, has_side_effects=True, vmem_limit_bytes=40 * 1024 * 1024
        ),
    )(*in_hbm)
    early, reward, late = pl.pallas_call(
        write_out,
        out_shape=tuple(pltpu.HBM(*shape) for shape in shapes),
        in_specs=[anywhere] * 3,
        out_specs=(anywhere,) * 3,
        scratch_shapes=[dma((3,))],
        compiler_params=pltpu.CompilerParams(vmem_limit_bytes=2 * 1024 * 1024),
    )(*(pltpu.with_memory_space_constraint(x, pltpu.VMEM) for x in staged))
    return early, reward.reshape(cand), late


def solution(mesh):
    groups, tn = mesh.shape["dp"], mesh.shape["tensor"]
    yn = min(RING, groups)
    placed = (
        P("dp", None, "tensor"),
        P("dp", None, "tensor"),
        P("dp"),
        P(None, "dp", "tensor"),
        P(None, "dp", "tensor"),
        P(None, "dp", "tensor"),
        P("tensor"),
        P("dp", None),
        P("dp", None),
        P("dp", None),
    )
    return jax.shard_map(
        functools.partial(local, (groups // yn, yn), tn),
        mesh=mesh,
        in_specs=placed,
        out_specs=(P(None, "dp", "tensor"), P("dp"), P(None, "dp", "tensor")),
        check_vma=False,
    )
```

```python
import functools
import math

import jax
import jax.numpy as jnp
from jax import lax
from jax.experimental import pallas as pl
from jax.experimental.pallas import tpu as pltpu
from jax.sharding import PartitionSpec as P

MESH = pl.DeviceIdType.MESH
HD = 128
PAD = 16
BLOCK = 8
RING = 8
NEG = -1e30
NT = (((1,), (1,)), ((), ()))


def all_of(ref, count, sem):
    part = ref.at[pl.ds(0, count)]
    return pltpu.make_async_copy(part, part, sem)


def kernel(
    dims,
    kept_h, lengths_h, cohort_h, place_h, weight_h,
    keys_h, values_h, queries_h, fresh_k_h, fresh_v_h,
    stage, reward_o, late_stage,
    kept_s, lengths_s, cohort_v, place_v, weight_v,
    kx, vx, qb, nkb, nvb, qf, nf, of, late_buf, send, recv,
    spread, row_v, idx_s, meta_mine, meta_all, rw,
    in_sem, row_sem, send_sem, recv_sem, meta_send, meta_recv, rw_send, rw_recv,
    ready_sem,
):
    zn, yn, tn, cand, kept_n, heads = dims
    groups = zn * yn
    cache = kx.shape[1] - PAD
    g_me = lax.axis_index("dp")
    t_me = lax.axis_index("tensor")
    z_me, y_me = g_me // yn, g_me % yn

    ins = [
        pltpu.make_async_copy(src, dst, in_sem.at[i])
        for i, (src, dst) in enumerate(
            (
                (cohort_h, cohort_v),
                (place_h, place_v),
                (fresh_k_h, nkb),
                (fresh_v_h, nvb),
                (queries_h, qb),
                (kept_h, kept_s),
                (lengths_h, lengths_s),
                (keys_h, kx.at[:, pl.ds(0, cache), :]),
                (values_h, vx.at[:, pl.ds(0, cache), :]),
                (weight_h, weight_v),
            )
        )
    ]
    for copy in ins:
        copy.start()

    barrier = pltpu.get_barrier_semaphore()

    def greet(g, _):
        pl.semaphore_signal(barrier, inc=1, device_id=(g, t_me), device_id_type=MESH)
        return 0

    lax.fori_loop(g_me + 1, groups, greet, 0)

    def greet_t(d, _):
        pl.semaphore_signal(
            barrier, inc=1, device_id=(g_me, lax.rem(t_me + d, tn)), device_id_type=MESH
        )
        return 0

    lax.fori_loop(1, tn, greet_t, 0)

    for copy in ins[:2]:
        copy.wait()

    eye = lax.broadcasted_iota(jnp.int32, (kept_n, kept_n), 0) == lax.broadcasted_iota(
        jnp.int32, (kept_n, kept_n), 1
    )

    def column(row):
        return jnp.sum(jnp.where(eye, row, 0), axis=1, keepdims=True)

    lane_g = lax.broadcasted_iota(jnp.int32, (kept_n, 128), 1)
    sub_k = lax.broadcasted_iota(jnp.int32, (kept_n, 128), 0)
    hit = column(cohort_v[...]) == lane_g
    chosen = jnp.min(jnp.where(hit, sub_k, kept_n), axis=0, keepdims=True)
    row_v[...] = chosen
    to_smem = pltpu.make_async_copy(row_v, idx_s, row_sem)
    to_smem.start()
    slot_of = jnp.max(
        jnp.where(
            cohort_v[...] == lax.broadcasted_iota(jnp.int32, (groups, kept_n), 0),
            place_v[...] + 1,
            0,
        ),
        axis=1,
        keepdims=True,
    )
    meta_mine[...] = jnp.broadcast_to(slot_of, (groups, 128)).reshape(groups, 1, 128)

    for copy in ins[2:5]:
        copy.wait()
    steps = qb.shape[0]

    def spread_queries(which):
        for t in which:
            for h in range(heads):
                qf[pl.ds((t * heads + h) * cand, cand), :] = qb[
                    t, :, h * HD : (h + 1) * HD
                ].astype(jnp.float32)

    spread_queries(range(steps // 2, steps))
    for which, source in enumerate((nkb, nvb)):
        for t in range(steps):
            nf[which, pl.ds(t * cand, cand), :] = source[t].astype(jnp.float32)
        nf[which, pl.ds(steps * cand, (8 - steps) * cand), :] = jnp.zeros(
            ((8 - steps) * cand, HD), jnp.float32
        )
    empty = jnp.zeros((PAD - 8, HD), jnp.float32)
    for c in range(cand):
        for which, target in enumerate((kx, vx)):
            rows = nf[which, pl.ds(c, 8, stride=cand), :]
            target[c, pl.ds(cache, PAD), :] = jnp.concatenate([rows, empty], axis=0).astype(
                jnp.bfloat16
            )
    for copy in ins[5:]:
        copy.wait()

    width = cache + PAD
    lane = lax.broadcasted_iota(jnp.int32, (2 * heads, width), 1)
    step_of_row = lax.broadcasted_iota(jnp.int32, (2 * heads, width), 0) // heads
    rate = math.log2(math.e) / math.sqrt(HD)

    def attend(cands, first_step):
        fresh_seen = (lane >= cache) & (lane <= cache + first_step + step_of_row)
        scores = []
        for c in cands:
            q = jnp.concatenate(
                [
                    qf[pl.ds((first_step + i) * heads * cand + c, heads, stride=cand), :]
                    for i in range(2)
                ],
                axis=0,
            ).astype(jnp.bfloat16)
            s = lax.dot_general(q, kx[c], NT, preferred_element_type=jnp.float32)
            scores.append(jnp.where((lane < lengths_s[c]) | fresh_seen, s, NEG))
        tops = [jnp.max(s, axis=1, keepdims=True) for s in scores]
        weights = [jnp.exp2((s - m) * rate) for s, m in zip(scores, tops)]
        totals = [jnp.sum(w, axis=1, keepdims=True) for w in weights]
        return [
            jnp.dot(w.astype(jnp.bfloat16), vx[c], preferred_element_type=jnp.float32)
            / total
            for c, w, total in zip(cands, weights, totals)
        ]

    def late_block(b, _):
        cands = [kept_s[0, b * BLOCK + j] for j in range(BLOCK)]
        outs = attend(cands, steps // 2)
        for j, o in enumerate(outs):
            late_buf[b * BLOCK + j] = o.astype(jnp.bfloat16)
        return 0

    late_buf[kept_n] = jnp.zeros(late_buf.shape[1:], jnp.bfloat16)
    lax.fori_loop(0, kept_n // BLOCK, late_block, 0)

    to_smem.wait()
    for g in range(groups):
        send[g] = late_buf[idx_s[0, g]]

    def send_to(g, _):
        for src, dst, sem_here, sem_there in (
            (meta_mine, meta_all, meta_send, meta_recv),
            (send, recv, send_sem, recv_sem),
        ):
            pltpu.make_async_remote_copy(
                src_ref=src.at[g],
                dst_ref=dst.at[g_me],
                send_sem=sem_here,
                recv_sem=sem_there,
                device_id=(g, t_me),
                device_id_type=MESH,
            ).start()
        return 0

    def tell(g, _):
        pl.semaphore_signal(
            ready_sem.at[z_me], inc=1, device_id=(g, t_me), device_id_type=MESH
        )
        return 0

    if tn > 1:
        pl.semaphore_wait(barrier, g_me + tn - 1)
    else:

        @pl.when(g_me > 0)
        def _():
            pl.semaphore_wait(barrier, g_me)

    def turn(j):
        return lax.rem(y_me + z_me + j, yn)

    def to_planes(*planes):
        for j in range(yn):
            for z in planes:
                send_to(z * yn + turn(j), 0)

    def to_plane(z, _):
        to_planes(z)
        return 0

    half = zn // 2

    @pl.when(z_me >= half)
    def _():
        for a in range(0, half, 2):
            to_planes(*range(a, min(a + 2, half)))

    lax.fori_loop(jnp.where(z_me >= half, half, 0), z_me, to_plane, 0)
    lax.fori_loop(z_me * yn, g_me, send_to, 0)
    lax.fori_loop(0, g_me, tell, 0)
    meta_all[g_me] = meta_mine[g_me]
    recv[g_me] = send[g_me]

    spread_queries(range(steps // 2))

    def early_block(b, _):
        cands = [b * BLOCK + j for j in range(BLOCK)]
        outs = attend(cands, 0)
        for c, o in zip(cands, outs):
            for i in range(2):
                of[pl.ds(i * heads * cand + c, heads, stride=cand), :] = o[
                    i * heads : (i + 1) * heads
                ]
        return 0

    lax.fori_loop(0, cand // BLOCK, early_block, 0)
    for t in range(2):
        for h in range(heads):
            stage[t, :, h * HD : (h + 1) * HD] = of[
                pl.ds((t * heads + h) * cand, cand), :
            ].astype(jnp.bfloat16)
    rw[t_me] = jnp.zeros(rw.shape[1:], jnp.float32)
    rw[t_me, :, pl.ds(0, cand)] = lax.dot_general(
        weight_v[...].reshape(1, heads * HD), stage[1], NT, preferred_element_type=jnp.float32
    )

    def rw_copy(d):
        return pltpu.make_async_remote_copy(
            src_ref=rw.at[t_me],
            dst_ref=rw.at[t_me],
            send_sem=rw_send,
            recv_sem=rw_recv,
            device_id=(g_me, lax.rem(t_me + d, tn)),
            device_id_type=MESH,
        )

    lax.fori_loop(1, tn, lambda d, _: (rw_copy(d).start(), 0)[1], 0)

    @pl.when(y_me < yn - 1)
    def _():
        pl.semaphore_wait(ready_sem.at[z_me], yn - 1 - y_me)
        lax.fori_loop(g_me + 1, (z_me + 1) * yn, send_to, 0)

    def later_plane(z, _):
        pl.semaphore_wait(ready_sem.at[z], yn)
        return to_plane(z, 0)

    lax.fori_loop(z_me + 1, zn, later_plane, 0)

    for sem in (meta_send, meta_recv):
        all_of(meta_all, groups - 1, sem).wait()
    slots_here = meta_all[...].reshape(groups, 128)[:, :kept_n]
    slot_ids = lax.broadcasted_iota(jnp.int32, (groups, kept_n), 1) + 1
    place = (slots_here == slot_ids).astype(jnp.float32).astype(jnp.bfloat16)
    all_of(recv, groups - 1, recv_sem).wait()
    spread[...] = recv[...].reshape(groups * 2 * heads, HD).astype(jnp.float32)
    for t in range(2):
        for h in range(heads):
            rows = spread[pl.ds(t * heads + h, groups, stride=2 * heads), :]
            late_stage[t, :, h * HD : (h + 1) * HD] = lax.dot_general(
                place,
                rows.astype(jnp.bfloat16),
                (((0,), (0,)), ((), ())),
                preferred_element_type=jnp.float32,
            ).astype(jnp.bfloat16)
    all_of(recv, groups - 1, send_sem).wait()
    if tn > 1:
        for sem in (rw_send, rw_recv):
            all_of(rw, tn - 1, sem).wait()
    reward_o[...] = jnp.sum(rw[...], axis=0)[:, :cand]


def write_out(early_v, reward_v, late_v, early_h, reward_h, late_h, sems):
    copies = [
        pltpu.make_async_copy(src, dst, sems.at[i])
        for i, (src, dst) in enumerate(
            ((early_v, early_h), (late_v, late_h), (reward_v, reward_h))
        )
    ]
    for copy in copies:
        copy.start()
    for copy in copies:
        copy.wait()


def local(
    ring,
    tn,
    cache_keys,
    cache_values,
    lengths,
    queries,
    new_keys,
    new_values,
    reward_weight,
    kept_candidates,
    arrival_cohort,
    arrival_place,
):
    zn, yn = ring
    groups = zn * yn
    cand, cache, _ = cache_keys.shape
    steps, _, columns = queries.shape
    heads = columns // HD
    kept_n = kept_candidates.shape[1]
    half = steps // 2
    bf16, f32, i32 = jnp.bfloat16, jnp.float32, jnp.int32
    anywhere = pl.BlockSpec(memory_space=pl.ANY)
    dma = pltpu.SemaphoreType.DMA
    shapes = (
        ((half, cand, columns), bf16),
        ((1, cand), f32),
        ((half, kept_n, columns), bf16),
    )
    in_hbm = [
        pltpu.with_memory_space_constraint(x, pltpu.HBM)
        for x in (
            kept_candidates,
            lengths,
            arrival_cohort,
            arrival_place,
            reward_weight,
            cache_keys,
            cache_values,
            queries,
            new_keys,
            new_values,
        )
    ]
    staged = pl.pallas_call(
        functools.partial(kernel, (zn, yn, tn, cand, kept_n, heads)),
        out_shape=tuple(pltpu.VMEM(*shape) for shape in shapes),
        in_specs=[anywhere] * len(in_hbm),
        out_specs=(pl.BlockSpec(memory_space=pltpu.VMEM),) * 3,
        scratch_shapes=[
            pltpu.SMEM(kept_candidates.shape, i32),
            pltpu.SMEM(lengths.shape, i32),
            pltpu.VMEM(arrival_cohort.shape, i32),
            pltpu.VMEM(arrival_place.shape, i32),
            pltpu.VMEM(reward_weight.shape, bf16),
            pltpu.VMEM((cand, cache + PAD, HD), bf16),
            pltpu.VMEM((cand, cache + PAD, HD), bf16),
            pltpu.VMEM(queries.shape, bf16),
            pltpu.VMEM(new_keys.shape, bf16),
            pltpu.VMEM(new_values.shape, bf16),
            pltpu.VMEM((steps * heads * cand, HD), f32),
            pltpu.VMEM((2, 8 * cand, HD), f32),
            pltpu.VMEM((half * heads * cand, HD), f32),
            pltpu.VMEM((kept_n + 1, half * heads, HD), bf16),
            pltpu.VMEM((groups, half * heads, HD), bf16),
            pltpu.VMEM((groups, half * heads, HD), bf16),
            pltpu.VMEM((groups * half * heads, HD), f32),
            pltpu.VMEM((1, 128), i32),
            pltpu.SMEM((1, 128), i32),
            pltpu.VMEM((groups, 1, 128), i32),
            pltpu.VMEM((groups, 1, 128), i32),
            pltpu.VMEM((tn, 1, 128), f32),
            dma((len(in_hbm),)), dma,
            dma, dma, dma, dma, dma, dma,
            pltpu.SemaphoreType.REGULAR((zn,)),
        ],
        compiler_params=pltpu.CompilerParams(
            collective_id=0, has_side_effects=True, vmem_limit_bytes=40 * 1024 * 1024
        ),
    )(*in_hbm)
    early, reward, late = pl.pallas_call(
        write_out,
        out_shape=tuple(pltpu.HBM(*shape) for shape in shapes),
        in_specs=[anywhere] * 3,
        out_specs=(anywhere,) * 3,
        scratch_shapes=[dma((3,))],
        compiler_params=pltpu.CompilerParams(vmem_limit_bytes=2 * 1024 * 1024),
    )(*(pltpu.with_memory_space_constraint(x, pltpu.VMEM) for x in staged))
    return early, reward.reshape(cand), late


def solution(mesh):
    groups, tn = mesh.shape["dp"], mesh.shape["tensor"]
    yn = min(RING, groups)
    placed = (
        P("dp", None, "tensor"),
        P("dp", None, "tensor"),
        P("dp"),
        P(None, "dp", "tensor"),
        P(None, "dp", "tensor"),
        P(None, "dp", "tensor"),
        P("tensor"),
        P("dp", None),
        P("dp", None),
        P("dp", None),
    )
    return jax.shard_map(
        functools.partial(local, (groups // yn, yn), tn),
        mesh=mesh,
        in_specs=placed,
        out_specs=(P(None, "dp", "tensor"), P("dp"), P(None, "dp", "tensor")),
        check_vma=False,
    )
```

```python
import functools
import math

import jax
import jax.numpy as jnp
from jax import lax
from jax.experimental import pallas as pl
from jax.experimental.pallas import tpu as pltpu
from jax.sharding import PartitionSpec as P

MESH = pl.DeviceIdType.MESH
HD = 128
PAD = 16
BLOCK = 16
RING = 8
NEG = -1e30
NT = (((1,), (1,)), ((), ()))


def all_of(ref, count, sem):
    part = ref.at[pl.ds(0, count)]
    return pltpu.make_async_copy(part, part, sem)


def kernel(
    dims,
    kept_h, lengths_h, cohort_h, place_h, weight_h,
    keys_h, values_h, queries_h, fresh_k_h, fresh_v_h,
    stage, reward_o, late_stage,
    kept_s, lengths_s, cohort_v, place_v, weight_v,
    kx, vx, qb, nkb, nvb, qf, nf, of, late_buf, send, recv,
    spread, row_v, idx_s, meta_mine, meta_all, rw,
    in_sem, row_sem, send_sem, recv_sem, meta_send, meta_recv, rw_send, rw_recv,
    ready_sem,
):
    zn, yn, tn, cand, kept_n, heads = dims
    groups = zn * yn
    cache = kx.shape[1] - PAD
    g_me = lax.axis_index("dp")
    t_me = lax.axis_index("tensor")
    z_me, y_me = g_me // yn, g_me % yn

    half = zn // 2
    depth = zn - half
    late = z_me >= half
    k_me = jnp.where(2 * y_me > yn, 2 * (yn - y_me), jnp.where(y_me > 0, 2 * y_me - 1, 0))
    r_me = jnp.where(late, half * yn + k_me * depth + z_me - half, g_me)
    b_me = jnp.where(late, half + k_me, z_me)
    k_next = jnp.where(late, k_me + 1, 0)

    def column_of(k, visit):
        y = jnp.where(lax.rem(k, 2) == 1, (k + 1) // 2, lax.rem(yn - k // 2, yn))
        for z in range(half, zn):
            visit(z * yn + y, 0)
        return 0

    def in_column(visit):
        return lambda z, _: visit(z * yn + y_me, 0)

    ins = [
        pltpu.make_async_copy(src, dst, in_sem.at[i])
        for i, (src, dst) in enumerate(
            (
                (cohort_h, cohort_v),
                (place_h, place_v),
                (fresh_k_h, nkb),
                (fresh_v_h, nvb),
                (queries_h, qb),
                (kept_h, kept_s),
                (lengths_h, lengths_s),
                (keys_h, kx.at[:, pl.ds(0, cache), :]),
                (values_h, vx.at[:, pl.ds(0, cache), :]),
                (weight_h, weight_v),
            )
        )
    ]
    for copy in ins:
        copy.start()

    barrier = pltpu.get_barrier_semaphore()

    def greet(g, _):
        pl.semaphore_signal(barrier, inc=1, device_id=(g, t_me), device_id_type=MESH)
        return 0

    lax.fori_loop(g_me + 1, jnp.where(late, g_me + 1, half * yn), greet, 0)
    lax.fori_loop(jnp.where(late, z_me + 1, zn), zn, in_column(greet), 0)
    lax.fori_loop(k_next, yn, lambda k, _: column_of(k, greet), 0)

    def greet_t(d, _):
        pl.semaphore_signal(
            barrier, inc=1, device_id=(g_me, lax.rem(t_me + d, tn)), device_id_type=MESH
        )
        return 0

    lax.fori_loop(1, tn, greet_t, 0)

    for copy in ins[:2]:
        copy.wait()

    eye = lax.broadcasted_iota(jnp.int32, (kept_n, kept_n), 0) == lax.broadcasted_iota(
        jnp.int32, (kept_n, kept_n), 1
    )

    def column(row):
        return jnp.sum(jnp.where(eye, row, 0), axis=1, keepdims=True)

    lane_g = lax.broadcasted_iota(jnp.int32, (kept_n, 128), 1)
    sub_k = lax.broadcasted_iota(jnp.int32, (kept_n, 128), 0)
    hit = column(cohort_v[...]) == lane_g
    chosen = jnp.min(jnp.where(hit, sub_k, kept_n), axis=0, keepdims=True)
    row_v[...] = chosen
    to_smem = pltpu.make_async_copy(row_v, idx_s, row_sem)
    to_smem.start()
    slot_of = jnp.max(
        jnp.where(
            cohort_v[...] == lax.broadcasted_iota(jnp.int32, (groups, kept_n), 0),
            place_v[...] + 1,
            0,
        ),
        axis=1,
        keepdims=True,
    )
    meta_mine[...] = jnp.broadcast_to(slot_of, (groups, 128)).reshape(groups, 1, 128)

    for copy in ins[2:5]:
        copy.wait()
    steps = qb.shape[0]

    def spread_queries(which):
        for t in which:
            for h in range(heads):
                qf[pl.ds((t * heads + h) * cand, cand), :] = qb[
                    t, :, h * HD : (h + 1) * HD
                ].astype(jnp.float32)

    spread_queries(range(steps // 2, steps))
    for which, source in enumerate((nkb, nvb)):
        for t in range(steps):
            nf[which, pl.ds(t * cand, cand), :] = source[t].astype(jnp.float32)
        nf[which, pl.ds(steps * cand, (8 - steps) * cand), :] = jnp.zeros(
            ((8 - steps) * cand, HD), jnp.float32
        )
    empty = jnp.zeros((PAD - 8, HD), jnp.float32)
    for c in range(cand):
        for which, target in enumerate((kx, vx)):
            rows = nf[which, pl.ds(c, 8, stride=cand), :]
            target[c, pl.ds(cache, PAD), :] = jnp.concatenate([rows, empty], axis=0).astype(
                jnp.bfloat16
            )
    for copy in ins[5:]:
        copy.wait()

    width = cache + PAD
    lane = lax.broadcasted_iota(jnp.int32, (2 * heads, width), 1)
    step_of_row = lax.broadcasted_iota(jnp.int32, (2 * heads, width), 0) // heads
    rate = math.log2(math.e) / math.sqrt(HD)

    def attend(cands, first_step):
        fresh_seen = (lane >= cache) & (lane <= cache + first_step + step_of_row)
        scores = []
        for c in cands:
            q = jnp.concatenate(
                [
                    qf[pl.ds((first_step + i) * heads * cand + c, heads, stride=cand), :]
                    for i in range(2)
                ],
                axis=0,
            ).astype(jnp.bfloat16)
            s = lax.dot_general(q, kx[c], NT, preferred_element_type=jnp.float32)
            scores.append(jnp.where((lane < lengths_s[c]) | fresh_seen, s, NEG))
        tops = [jnp.max(s, axis=1, keepdims=True) for s in scores]
        weights = [jnp.exp2((s - m) * rate) for s, m in zip(scores, tops)]
        totals = [jnp.sum(w, axis=1, keepdims=True) for w in weights]
        return [
            jnp.dot(w.astype(jnp.bfloat16), vx[c], preferred_element_type=jnp.float32)
            / total
            for c, w, total in zip(cands, weights, totals)
        ]

    def late_block(b, _):
        cands = [kept_s[0, b * BLOCK + j] for j in range(BLOCK)]
        outs = attend(cands, steps // 2)
        for j, o in enumerate(outs):
            late_buf[b * BLOCK + j] = o.astype(jnp.bfloat16)
        return 0

    late_buf[kept_n] = jnp.zeros(late_buf.shape[1:], jnp.bfloat16)
    lax.fori_loop(0, kept_n // BLOCK, late_block, 0)

    to_smem.wait()
    for g in range(groups):
        send[g] = late_buf[idx_s[0, g]]

    def send_to(g, _):
        for src, dst, sem_here, sem_there in (
            (meta_mine, meta_all, meta_send, meta_recv),
            (send, recv, send_sem, recv_sem),
        ):
            pltpu.make_async_remote_copy(
                src_ref=src.at[g],
                dst_ref=dst.at[g_me],
                send_sem=sem_here,
                recv_sem=sem_there,
                device_id=(g, t_me),
                device_id_type=MESH,
            ).start()
        return 0

    def tell(g, _):
        pl.semaphore_signal(
            ready_sem.at[b_me], inc=1, device_id=(g, t_me), device_id_type=MESH
        )
        return 0

    if tn > 1:
        pl.semaphore_wait(barrier, r_me + tn - 1)
    else:

        @pl.when(r_me > 0)
        def _():
            pl.semaphore_wait(barrier, r_me)

    def turn(j):
        return lax.rem(y_me + z_me + j, yn)

    def to_planes(*planes):
        for j in range(yn):
            for z in planes:
                send_to(z * yn + turn(j), 0)

    def to_plane(z, _):
        to_planes(z)
        return 0

    @pl.when(late)
    def _():
        for a in range(half):
            to_planes(a)

    lax.fori_loop(0, jnp.where(late, 0, z_me), to_plane, 0)
    lax.fori_loop(jnp.where(late, g_me, z_me * yn), g_me, send_to, 0)
    lax.fori_loop(0, k_next - 1, lambda k, _: column_of(k, send_to), 0)
    lax.fori_loop(half, jnp.where(late, z_me, half), in_column(send_to), 0)

    lax.fori_loop(0, jnp.where(late, half * yn, g_me), tell, 0)
    lax.fori_loop(0, k_next - 1, lambda k, _: column_of(k, tell), 0)
    lax.fori_loop(half, jnp.where(late, z_me, half), in_column(tell), 0)
    meta_all[g_me] = meta_mine[g_me]
    recv[g_me] = send[g_me]

    spread_queries(range(steps // 2))

    def early_block(b, _):
        cands = [b * BLOCK + j for j in range(BLOCK)]
        outs = attend(cands, 0)
        for c, o in zip(cands, outs):
            for i in range(2):
                of[pl.ds(i * heads * cand + c, heads, stride=cand), :] = o[
                    i * heads : (i + 1) * heads
                ]
        return 0

    lax.fori_loop(0, cand // BLOCK, early_block, 0)
    for t in range(2):
        for h in range(heads):
            stage[t, :, h * HD : (h + 1) * HD] = of[
                pl.ds((t * heads + h) * cand, cand), :
            ].astype(jnp.bfloat16)
    rw[t_me] = jnp.zeros(rw.shape[1:], jnp.float32)
    rw[t_me, :, pl.ds(0, cand)] = lax.dot_general(
        weight_v[...].reshape(1, heads * HD), stage[1], NT, preferred_element_type=jnp.float32
    )

    def rw_copy(d):
        return pltpu.make_async_remote_copy(
            src_ref=rw.at[t_me],
            dst_ref=rw.at[t_me],
            send_sem=rw_send,
            recv_sem=rw_recv,
            device_id=(g_me, lax.rem(t_me + d, tn)),
            device_id_type=MESH,
        )

    lax.fori_loop(1, tn, lambda d, _: (rw_copy(d).start(), 0)[1], 0)

    @pl.when(jnp.logical_not(late))
    def _():
        @pl.when(y_me < yn - 1)
        def _():
            pl.semaphore_wait(ready_sem.at[z_me], yn - 1 - y_me)
            lax.fori_loop(g_me + 1, (z_me + 1) * yn, send_to, 0)

        def later_plane(z, _):
            pl.semaphore_wait(ready_sem.at[z], yn)
            return to_plane(z, 0)

        lax.fori_loop(z_me + 1, half, later_plane, 0)

    @pl.when(late & (z_me < zn - 1))
    def _():
        pl.semaphore_wait(ready_sem.at[half + k_me], zn - 1 - z_me)
        lax.fori_loop(z_me + 1, zn, in_column(send_to), 0)

    def later_column(k, _):
        pl.semaphore_wait(ready_sem.at[half + k], depth)
        return column_of(k, send_to)

    lax.fori_loop(k_next, yn, later_column, 0)

    for sem in (meta_send, meta_recv):
        all_of(meta_all, groups - 1, sem).wait()
    slots_here = meta_all[...].reshape(groups, 128)[:, :kept_n]
    slot_ids = lax.broadcasted_iota(jnp.int32, (groups, kept_n), 1) + 1
    place = (slots_here == slot_ids).astype(jnp.float32).astype(jnp.bfloat16)
    all_of(recv, groups - 1, recv_sem).wait()
    spread[...] = recv[...].reshape(groups * 2 * heads, HD).astype(jnp.float32)
    for t in range(2):
        for h in range(heads):
            rows = spread[pl.ds(t * heads + h, groups, stride=2 * heads), :]
            late_stage[t, :, h * HD : (h + 1) * HD] = lax.dot_general(
                place,
                rows.astype(jnp.bfloat16),
                (((0,), (0,)), ((), ())),
                preferred_element_type=jnp.float32,
            ).astype(jnp.bfloat16)
    all_of(recv, groups - 1, send_sem).wait()
    if tn > 1:
        for sem in (rw_send, rw_recv):
            all_of(rw, tn - 1, sem).wait()
    reward_o[...] = jnp.sum(rw[...], axis=0)[:, :cand]


def write_out(early_v, reward_v, late_v, early_h, reward_h, late_h, sems):
    copies = [
        pltpu.make_async_copy(src, dst, sems.at[i])
        for i, (src, dst) in enumerate(
            ((early_v, early_h), (late_v, late_h), (reward_v, reward_h))
        )
    ]
    for copy in copies:
        copy.start()
    for copy in copies:
        copy.wait()


def local(
    ring,
    tn,
    cache_keys,
    cache_values,
    lengths,
    queries,
    new_keys,
    new_values,
    reward_weight,
    kept_candidates,
    arrival_cohort,
    arrival_place,
):
    zn, yn = ring
    groups = zn * yn
    cand, cache, _ = cache_keys.shape
    steps, _, columns = queries.shape
    heads = columns // HD
    kept_n = kept_candidates.shape[1]
    half = steps // 2
    bf16, f32, i32 = jnp.bfloat16, jnp.float32, jnp.int32
    anywhere = pl.BlockSpec(memory_space=pl.ANY)
    dma = pltpu.SemaphoreType.DMA
    shapes = (
        ((half, cand, columns), bf16),
        ((1, cand), f32),
        ((half, kept_n, columns), bf16),
    )
    in_hbm = [
        pltpu.with_memory_space_constraint(x, pltpu.HBM)
        for x in (
            kept_candidates,
            lengths,
            arrival_cohort,
            arrival_place,
            reward_weight,
            cache_keys,
            cache_values,
            queries,
            new_keys,
            new_values,
        )
    ]
    staged = pl.pallas_call(
        functools.partial(kernel, (zn, yn, tn, cand, kept_n, heads)),
        out_shape=tuple(pltpu.VMEM(*shape) for shape in shapes),
        in_specs=[anywhere] * len(in_hbm),
        out_specs=(pl.BlockSpec(memory_space=pltpu.VMEM),) * 3,
        scratch_shapes=[
            pltpu.SMEM(kept_candidates.shape, i32),
            pltpu.SMEM(lengths.shape, i32),
            pltpu.VMEM(arrival_cohort.shape, i32),
            pltpu.VMEM(arrival_place.shape, i32),
            pltpu.VMEM(reward_weight.shape, bf16),
            pltpu.VMEM((cand, cache + PAD, HD), bf16),
            pltpu.VMEM((cand, cache + PAD, HD), bf16),
            pltpu.VMEM(queries.shape, bf16),
            pltpu.VMEM(new_keys.shape, bf16),
            pltpu.VMEM(new_values.shape, bf16),
            pltpu.VMEM((steps * heads * cand, HD), f32),
            pltpu.VMEM((2, 8 * cand, HD), f32),
            pltpu.VMEM((half * heads * cand, HD), f32),
            pltpu.VMEM((kept_n + 1, half * heads, HD), bf16),
            pltpu.VMEM((groups, half * heads, HD), bf16),
            pltpu.VMEM((groups, half * heads, HD), bf16),
            pltpu.VMEM((groups * half * heads, HD), f32),
            pltpu.VMEM((1, 128), i32),
            pltpu.SMEM((1, 128), i32),
            pltpu.VMEM((groups, 1, 128), i32),
            pltpu.VMEM((groups, 1, 128), i32),
            pltpu.VMEM((tn, 1, 128), f32),
            dma((len(in_hbm),)), dma,
            dma, dma, dma, dma, dma, dma,
            pltpu.SemaphoreType.REGULAR((zn // 2 + yn,)),
        ],
        compiler_params=pltpu.CompilerParams(
            collective_id=0, has_side_effects=True, vmem_limit_bytes=40 * 1024 * 1024
        ),
    )(*in_hbm)
    early, reward, late = pl.pallas_call(
        write_out,
        out_shape=tuple(pltpu.HBM(*shape) for shape in shapes),
        in_specs=[anywhere] * 3,
        out_specs=(anywhere,) * 3,
        scratch_shapes=[dma((3,))],
        compiler_params=pltpu.CompilerParams(vmem_limit_bytes=2 * 1024 * 1024),
    )(*(pltpu.with_memory_space_constraint(x, pltpu.VMEM) for x in staged))
    return early, reward.reshape(cand), late


def solution(mesh):
    groups, tn = mesh.shape["dp"], mesh.shape["tensor"]
    yn = min(RING, groups)
    placed = (
        P("dp", None, "tensor"),
        P("dp", None, "tensor"),
        P("dp"),
        P(None, "dp", "tensor"),
        P(None, "dp", "tensor"),
        P(None, "dp", "tensor"),
        P("tensor"),
        P("dp", None),
        P("dp", None),
        P("dp", None),
    )
    return jax.shard_map(
        functools.partial(local, (groups // yn, yn), tn),
        mesh=mesh,
        in_specs=placed,
        out_specs=(P(None, "dp", "tensor"), P("dp"), P(None, "dp", "tensor")),
        check_vma=False,
    )
```

```python
import functools
import math

import jax
import jax.numpy as jnp
from jax import lax
from jax.experimental import pallas as pl
from jax.experimental.pallas import tpu as pltpu
from jax.sharding import PartitionSpec as P

MESH = pl.DeviceIdType.MESH
HD = 128
PAD = 16
BLOCK = 16
RING = 8
NEG = -1e30
NT = (((1,), (1,)), ((), ()))


def all_of(ref, count, sem):
    part = ref.at[pl.ds(0, count)]
    return pltpu.make_async_copy(part, part, sem)


def kernel(
    dims,
    kept_h, lengths_h, cohort_h, place_h, weight_h,
    keys_h, values_h, queries_h, fresh_k_h, fresh_v_h,
    stage, reward_o, late_stage,
    kept_s, lengths_s, cohort_v, place_v, weight_v,
    kx, vx, qb, nkb, nvb, qf, nf, of, late_buf, send, recv,
    spread, row_v, idx_s, meta_mine, meta_all, rw,
    in_sem, row_sem, send_sem, recv_sem, meta_send, meta_recv, rw_send, rw_recv,
    ready_sem, peer_sem,
):
    zn, yn, tn, cand, kept_n, heads = dims
    groups = zn * yn
    cache = kx.shape[1] - PAD
    g_me = lax.axis_index("dp")
    t_me = lax.axis_index("tensor")
    z_me, y_me = g_me // yn, g_me % yn

    half = zn // 2
    depth = zn - half
    late = z_me >= half
    k_me = jnp.where(2 * y_me > yn, 2 * (yn - y_me), jnp.where(y_me > 0, 2 * y_me - 1, 0))
    r_me = jnp.where(late, half * yn + k_me * depth + z_me - half, g_me)
    b_me = jnp.where(late, half + k_me, z_me)
    k_next = jnp.where(late, k_me + 1, 0)

    def column_of(k, visit):
        y = jnp.where(lax.rem(k, 2) == 1, (k + 1) // 2, lax.rem(yn - k // 2, yn))
        for z in range(half, zn):
            visit(z * yn + y, 0)
        return 0

    def in_column(visit):
        return lambda z, _: visit(z * yn + y_me, 0)

    ins = [
        pltpu.make_async_copy(src, dst, in_sem.at[i])
        for i, (src, dst) in enumerate(
            (
                (cohort_h, cohort_v),
                (place_h, place_v),
                (fresh_k_h, nkb),
                (fresh_v_h, nvb),
                (queries_h, qb),
                (kept_h, kept_s),
                (lengths_h, lengths_s),
                (keys_h, kx.at[:, pl.ds(0, cache), :]),
                (values_h, vx.at[:, pl.ds(0, cache), :]),
                (weight_h, weight_v),
            )
        )
    ]
    for copy in ins:
        copy.start()

    pairs = (tn + 1) // 2
    p_me = lax.rem(t_me, 2) * pairs + t_me // 2

    def peer(p):
        return (g_me, lax.rem(p, pairs) * 2 + p // pairs)

    barrier = pltpu.get_barrier_semaphore()

    def greet(g, _):
        pl.semaphore_signal(barrier, inc=1, device_id=(g, t_me), device_id_type=MESH)
        return 0

    lax.fori_loop(g_me + 1, jnp.where(late, g_me + 1, half * yn), greet, 0)
    lax.fori_loop(jnp.where(late, z_me + 1, zn), zn, in_column(greet), 0)
    lax.fori_loop(k_next, yn, lambda k, _: column_of(k, greet), 0)

    def greet_peer(p, _):
        pl.semaphore_signal(barrier, inc=1, device_id=peer(p), device_id_type=MESH)
        return 0

    lax.fori_loop(p_me + 1, tn, greet_peer, 0)

    for copy in ins[:2]:
        copy.wait()

    eye = lax.broadcasted_iota(jnp.int32, (kept_n, kept_n), 0) == lax.broadcasted_iota(
        jnp.int32, (kept_n, kept_n), 1
    )

    def column(row):
        return jnp.sum(jnp.where(eye, row, 0), axis=1, keepdims=True)

    lane_g = lax.broadcasted_iota(jnp.int32, (kept_n, 128), 1)
    sub_k = lax.broadcasted_iota(jnp.int32, (kept_n, 128), 0)
    hit = column(cohort_v[...]) == lane_g
    chosen = jnp.min(jnp.where(hit, sub_k, kept_n), axis=0, keepdims=True)
    row_v[...] = chosen
    to_smem = pltpu.make_async_copy(row_v, idx_s, row_sem)
    to_smem.start()
    slot_of = jnp.max(
        jnp.where(
            cohort_v[...] == lax.broadcasted_iota(jnp.int32, (groups, kept_n), 0),
            place_v[...] + 1,
            0,
        ),
        axis=1,
        keepdims=True,
    )
    meta_mine[...] = jnp.broadcast_to(slot_of, (groups, 128)).reshape(groups, 1, 128)

    for copy in ins[2:5]:
        copy.wait()
    steps = qb.shape[0]

    def spread_queries(which):
        for t in which:
            for h in range(heads):
                qf[pl.ds((t * heads + h) * cand, cand), :] = qb[
                    t, :, h * HD : (h + 1) * HD
                ].astype(jnp.float32)

    spread_queries(range(steps // 2, steps))
    for which, source in enumerate((nkb, nvb)):
        for t in range(steps):
            nf[which, pl.ds(t * cand, cand), :] = source[t].astype(jnp.float32)
        nf[which, pl.ds(steps * cand, (8 - steps) * cand), :] = jnp.zeros(
            ((8 - steps) * cand, HD), jnp.float32
        )
    empty = jnp.zeros((PAD - 8, HD), jnp.float32)
    for c in range(cand):
        for which, target in enumerate((kx, vx)):
            rows = nf[which, pl.ds(c, 8, stride=cand), :]
            target[c, pl.ds(cache, PAD), :] = jnp.concatenate([rows, empty], axis=0).astype(
                jnp.bfloat16
            )
    for copy in ins[5:]:
        copy.wait()

    width = cache + PAD
    lane = lax.broadcasted_iota(jnp.int32, (2 * heads, width), 1)
    step_of_row = lax.broadcasted_iota(jnp.int32, (2 * heads, width), 0) // heads
    rate = math.log2(math.e) / math.sqrt(HD)

    def attend(cands, first_step):
        fresh_seen = (lane >= cache) & (lane <= cache + first_step + step_of_row)
        scores = []
        for c in cands:
            q = jnp.concatenate(
                [
                    qf[pl.ds((first_step + i) * heads * cand + c, heads, stride=cand), :]
                    for i in range(2)
                ],
                axis=0,
            ).astype(jnp.bfloat16)
            s = lax.dot_general(q, kx[c], NT, preferred_element_type=jnp.float32)
            scores.append(jnp.where((lane < lengths_s[c]) | fresh_seen, s, NEG))
        tops = [jnp.max(s, axis=1, keepdims=True) for s in scores]
        weights = [jnp.exp2((s - m) * rate) for s, m in zip(scores, tops)]
        totals = [jnp.sum(w, axis=1, keepdims=True) for w in weights]
        return [
            jnp.dot(w.astype(jnp.bfloat16), vx[c], preferred_element_type=jnp.float32)
            / total
            for c, w, total in zip(cands, weights, totals)
        ]

    def late_block(b, _):
        cands = [kept_s[0, b * BLOCK + j] for j in range(BLOCK)]
        outs = attend(cands, steps // 2)
        for j, o in enumerate(outs):
            late_buf[b * BLOCK + j] = o.astype(jnp.bfloat16)
        return 0

    late_buf[kept_n] = jnp.zeros(late_buf.shape[1:], jnp.bfloat16)
    lax.fori_loop(0, kept_n // BLOCK, late_block, 0)

    to_smem.wait()
    for g in range(groups):
        send[g] = late_buf[idx_s[0, g]]

    def send_to(g, _):
        for src, dst, sem_here, sem_there in (
            (meta_mine, meta_all, meta_send, meta_recv),
            (send, recv, send_sem, recv_sem),
        ):
            pltpu.make_async_remote_copy(
                src_ref=src.at[g],
                dst_ref=dst.at[g_me],
                send_sem=sem_here,
                recv_sem=sem_there,
                device_id=(g, t_me),
                device_id_type=MESH,
            ).start()
        return 0

    def tell(g, _):
        pl.semaphore_signal(
            ready_sem.at[b_me], inc=1, device_id=(g, t_me), device_id_type=MESH
        )
        return 0

    @pl.when(r_me + p_me > 0)
    def _():
        pl.semaphore_wait(barrier, r_me + p_me)

    def turn(j):
        return lax.rem(y_me + z_me + j, yn)

    def to_planes(*planes):
        for j in range(yn):
            for z in planes:
                send_to(z * yn + turn(j), 0)

    def to_plane(z, _):
        to_planes(z)
        return 0

    @pl.when(late)
    def _():
        for a in range(half):
            to_planes(a)

    lax.fori_loop(0, jnp.where(late, 0, z_me), to_plane, 0)
    lax.fori_loop(jnp.where(late, g_me, z_me * yn), g_me, send_to, 0)
    lax.fori_loop(0, k_next - 1, lambda k, _: column_of(k, send_to), 0)
    lax.fori_loop(half, jnp.where(late, z_me, half), in_column(send_to), 0)

    lax.fori_loop(0, jnp.where(late, half * yn, g_me), tell, 0)
    lax.fori_loop(0, k_next - 1, lambda k, _: column_of(k, tell), 0)
    lax.fori_loop(half, jnp.where(late, z_me, half), in_column(tell), 0)
    def tell_peer(p, _):
        pl.semaphore_signal(peer_sem, inc=1, device_id=peer(p), device_id_type=MESH)
        return 0

    lax.fori_loop(0, p_me, tell_peer, 0)
    meta_all[g_me] = meta_mine[g_me]
    recv[g_me] = send[g_me]

    spread_queries(range(steps // 2))

    def early_block(b, _):
        cands = [b * BLOCK + j for j in range(BLOCK)]
        outs = attend(cands, 0)
        for c, o in zip(cands, outs):
            for i in range(2):
                of[pl.ds(i * heads * cand + c, heads, stride=cand), :] = o[
                    i * heads : (i + 1) * heads
                ]
        return 0

    lax.fori_loop(0, cand // BLOCK, early_block, 0)
    for t in range(2):
        for h in range(heads):
            stage[t, :, h * HD : (h + 1) * HD] = of[
                pl.ds((t * heads + h) * cand, cand), :
            ].astype(jnp.bfloat16)
    rw[t_me] = jnp.zeros(rw.shape[1:], jnp.float32)
    rw[t_me, :, pl.ds(0, cand)] = lax.dot_general(
        weight_v[...].reshape(1, heads * HD), stage[1], NT, preferred_element_type=jnp.float32
    )

    def send_reward(p, _):
        pltpu.make_async_remote_copy(
            src_ref=rw.at[t_me],
            dst_ref=rw.at[t_me],
            send_sem=rw_send,
            recv_sem=rw_recv,
            device_id=peer(p),
            device_id_type=MESH,
        ).start()
        return 0

    lax.fori_loop(0, p_me, send_reward, 0)

    @pl.when(p_me < tn - 1)
    def _():
        pl.semaphore_wait(peer_sem, tn - 1 - p_me)
        lax.fori_loop(p_me + 1, tn, send_reward, 0)

    @pl.when(jnp.logical_not(late))
    def _():
        @pl.when(y_me < yn - 1)
        def _():
            pl.semaphore_wait(ready_sem.at[z_me], yn - 1 - y_me)
            lax.fori_loop(g_me + 1, (z_me + 1) * yn, send_to, 0)

        def later_plane(z, _):
            pl.semaphore_wait(ready_sem.at[z], yn)
            return to_plane(z, 0)

        lax.fori_loop(z_me + 1, half, later_plane, 0)

    @pl.when(late & (z_me < zn - 1))
    def _():
        pl.semaphore_wait(ready_sem.at[half + k_me], zn - 1 - z_me)
        lax.fori_loop(z_me + 1, zn, in_column(send_to), 0)

    def later_column(k, _):
        pl.semaphore_wait(ready_sem.at[half + k], depth)
        return column_of(k, send_to)

    lax.fori_loop(k_next, yn, later_column, 0)

    for sem in (meta_send, meta_recv):
        all_of(meta_all, groups - 1, sem).wait()
    slots_here = meta_all[...].reshape(groups, 128)[:, :kept_n]
    slot_ids = lax.broadcasted_iota(jnp.int32, (groups, kept_n), 1) + 1
    place = (slots_here == slot_ids).astype(jnp.float32).astype(jnp.bfloat16)
    all_of(recv, groups - 1, recv_sem).wait()
    spread[...] = recv[...].reshape(groups * 2 * heads, HD).astype(jnp.float32)
    for t in range(2):
        for h in range(heads):
            rows = spread[pl.ds(t * heads + h, groups, stride=2 * heads), :]
            late_stage[t, :, h * HD : (h + 1) * HD] = lax.dot_general(
                place,
                rows.astype(jnp.bfloat16),
                (((0,), (0,)), ((), ())),
                preferred_element_type=jnp.float32,
            ).astype(jnp.bfloat16)
    all_of(recv, groups - 1, send_sem).wait()
    if tn > 1:
        for sem in (rw_send, rw_recv):
            all_of(rw, tn - 1, sem).wait()
    reward_o[...] = jnp.sum(rw[...], axis=0)[:, :cand]


def write_out(early_v, reward_v, late_v, early_h, reward_h, late_h, sems):
    copies = [
        pltpu.make_async_copy(src, dst, sems.at[i])
        for i, (src, dst) in enumerate(
            ((early_v, early_h), (late_v, late_h), (reward_v, reward_h))
        )
    ]
    for copy in copies:
        copy.start()
    for copy in copies:
        copy.wait()


def local(
    ring,
    tn,
    cache_keys,
    cache_values,
    lengths,
    queries,
    new_keys,
    new_values,
    reward_weight,
    kept_candidates,
    arrival_cohort,
    arrival_place,
):
    zn, yn = ring
    groups = zn * yn
    cand, cache, _ = cache_keys.shape
    steps, _, columns = queries.shape
    heads = columns // HD
    kept_n = kept_candidates.shape[1]
    half = steps // 2
    bf16, f32, i32 = jnp.bfloat16, jnp.float32, jnp.int32
    anywhere = pl.BlockSpec(memory_space=pl.ANY)
    dma = pltpu.SemaphoreType.DMA
    shapes = (
        ((half, cand, columns), bf16),
        ((1, cand), f32),
        ((half, kept_n, columns), bf16),
    )
    in_hbm = [
        pltpu.with_memory_space_constraint(x, pltpu.HBM)
        for x in (
            kept_candidates,
            lengths,
            arrival_cohort,
            arrival_place,
            reward_weight,
            cache_keys,
            cache_values,
            queries,
            new_keys,
            new_values,
        )
    ]
    staged = pl.pallas_call(
        functools.partial(kernel, (zn, yn, tn, cand, kept_n, heads)),
        out_shape=tuple(pltpu.VMEM(*shape) for shape in shapes),
        in_specs=[anywhere] * len(in_hbm),
        out_specs=(pl.BlockSpec(memory_space=pltpu.VMEM),) * 3,
        scratch_shapes=[
            pltpu.SMEM(kept_candidates.shape, i32),
            pltpu.SMEM(lengths.shape, i32),
            pltpu.VMEM(arrival_cohort.shape, i32),
            pltpu.VMEM(arrival_place.shape, i32),
            pltpu.VMEM(reward_weight.shape, bf16),
            pltpu.VMEM((cand, cache + PAD, HD), bf16),
            pltpu.VMEM((cand, cache + PAD, HD), bf16),
            pltpu.VMEM(queries.shape, bf16),
            pltpu.VMEM(new_keys.shape, bf16),
            pltpu.VMEM(new_values.shape, bf16),
            pltpu.VMEM((steps * heads * cand, HD), f32),
            pltpu.VMEM((2, 8 * cand, HD), f32),
            pltpu.VMEM((half * heads * cand, HD), f32),
            pltpu.VMEM((kept_n + 1, half * heads, HD), bf16),
            pltpu.VMEM((groups, half * heads, HD), bf16),
            pltpu.VMEM((groups, half * heads, HD), bf16),
            pltpu.VMEM((groups * half * heads, HD), f32),
            pltpu.VMEM((1, 128), i32),
            pltpu.SMEM((1, 128), i32),
            pltpu.VMEM((groups, 1, 128), i32),
            pltpu.VMEM((groups, 1, 128), i32),
            pltpu.VMEM((tn, 1, 128), f32),
            dma((len(in_hbm),)), dma,
            dma, dma, dma, dma, dma, dma,
            pltpu.SemaphoreType.REGULAR((zn // 2 + yn,)),
            pltpu.SemaphoreType.REGULAR,
        ],
        compiler_params=pltpu.CompilerParams(
            collective_id=0, has_side_effects=True, vmem_limit_bytes=40 * 1024 * 1024
        ),
    )(*in_hbm)
    early, reward, late = pl.pallas_call(
        write_out,
        out_shape=tuple(pltpu.HBM(*shape) for shape in shapes),
        in_specs=[anywhere] * 3,
        out_specs=(anywhere,) * 3,
        scratch_shapes=[dma((3,))],
        compiler_params=pltpu.CompilerParams(vmem_limit_bytes=2 * 1024 * 1024),
    )(*(pltpu.with_memory_space_constraint(x, pltpu.VMEM) for x in staged))
    return early, reward.reshape(cand), late


def solution(mesh):
    groups, tn = mesh.shape["dp"], mesh.shape["tensor"]
    yn = min(RING, groups)
    placed = (
        P("dp", None, "tensor"),
        P("dp", None, "tensor"),
        P("dp"),
        P(None, "dp", "tensor"),
        P(None, "dp", "tensor"),
        P(None, "dp", "tensor"),
        P("tensor"),
        P("dp", None),
        P("dp", None),
        P("dp", None),
    )
    return jax.shard_map(
        functools.partial(local, (groups // yn, yn), tn),
        mesh=mesh,
        in_specs=placed,
        out_specs=(P(None, "dp", "tensor"), P("dp"), P(None, "dp", "tensor")),
        check_vma=False,
    )
```
